32 devices in a mesh: leaf: 2 (over x), prow: 4 (over z), pcol: 4 (over y, core).
Axes of the slice: x: 2, y: 2, z: 4, core: 2. Of those that a mesh axis runs over, the one named last changes fastest.
Arguments:
- subtree_factor: float32 [2, 2, 8, 256, 2048], P('leaf', None, None, 'prow', 'pcol'), may hold values from -0.09375 to 0.09375
- sub_linv: float32 [2, 2, 8, 256, 256], P('leaf', None, None, 'prow'), may hold values from -0.05 to 1.05
- sub_uinv: float32 [2, 2, 8, 256, 256], P('leaf', None, None, 'prow'), may hold values from -0.05 to 1.05
- lower_panel: float32 [2, 4, 256, 2, 2048], P('leaf', None, 'prow', None, 'pcol'), may hold values from -0.046875 to 0.046875
- upper_panel: float32 [2, 2, 8, 256, 1024], P('leaf', None, None, 'prow', 'pcol'), may hold values from -0.125 to 0.125
- panel_rows: int32 [2, 4, 2], P('leaf'), may hold values 0 or 1
- upper_level_factor: float32 [4, 256, 1024], P(None, 'prow', 'pcol'), may hold values from -0.125 to 0.125
- top_linv: float32 [4, 256, 256], P(None, 'prow'), may hold values from -0.05 to 1.05
- top_uinv: float32 [4, 256, 256], P(None, 'prow'), may hold values from -0.05 to 1.05
- sub_rhs: float32 [2, 2, 8, 256, 256], P('leaf', None, None, 'prow'), may hold values from -6 to 6
- top_rhs: float32 [4, 256, 256], P(None, 'prow', 'leaf'), may hold values from -6 to 6
Outputs:
- sub_solution: float32 [2, 2, 8, 256, 256], P('leaf', None, 'pcol')
- top_solution: float32 [4, 256, 256], P('pcol', None, 'leaf')
The draws below stay inside these ranges and needn't reach their ends.
All inputs are finite; a program needn't handle non-finite values. No bound on the sum of `panel_rows` on one device may be relied on, other than what follows from the above.
Results may differ from the reference program's by a relative error of at most 0.00013.
Values sent between devices are 32-bit elements; how exact they have to be, the bound alone decides.
No kernel may reach another device: no remote copies, remote signals or barrier semaphores. Data moves between devices by JAX's collectives and lax.ppermute only.
A program may use at most 128 MiB of HBM per device.

```python
import jax
import jax.numpy as jnp
from jax import lax

NB = 256
NR = 256
SUB = 2
NS = 8
NT = 4
LAYERS = 2


def near_identity(key, leading):
    spread = jax.random.uniform(key, leading + (NB, NB), jnp.float32, -0.05, 0.05)
    return spread + jnp.eye(NB, dtype=jnp.float32)


def draw_sub_linv(key, part):
    return near_identity(jax.random.fold_in(key, 11), (LAYERS, SUB, NS))


def draw_sub_uinv(key, part):
    return near_identity(jax.random.fold_in(key, 23), (LAYERS, SUB, NS))


def draw_top_linv(key, part):
    return near_identity(jax.random.fold_in(key, 37), (NT,))


def draw_top_uinv(key, part):
    return near_identity(jax.random.fold_in(key, 41), (NT,))


def touch_ends(values, stream_key, least, high):
    longest = values.shape.index(max(values.shape))
    spots = []
    for shift in (0, 1):
        where = [jax.random.randint(jax.random.fold_in(stream_key, axis), (), 0, length) for axis, length in enumerate(values.shape)]
        where[longest] = (where[longest] + shift) % values.shape[longest]
        spots.append(tuple(where))
    return values.at[spots[0]].set(least).at[spots[1]].set(high)


def shard_levels(rng, extent, shards, least, top_value):
    def one(position, parts):
        heights = jax.random.uniform(jax.random.fold_in(jax.random.fold_in(rng, 6), position), (parts,), jnp.float32, least / len(shards), top_value / len(shards))
        return jnp.repeat(jnp.exp(heights), extent[position] // parts).reshape((-1,) + (1,) * (len(extent) - position - 1))

    loudness = one(*shards[0])
    for cut in shards[1:]:
        loudness = loudness * one(*cut)
    return loudness


def gaussian(stream_key, extent, scale, bound, cuts=(), held_as=jnp.bfloat16):
    entries = scale * jax.random.normal(stream_key, extent, jnp.float32)
    if cuts:
        entries = entries * shard_levels(stream_key, extent, cuts, -0.22, 0.18)
    return jnp.clip(entries, -bound, bound).astype(held_as)


def setup_inputs(seed: int = 0) -> dict:
    key_list = jax.random.split(jax.random.key(seed), 12)
    return {
        "subtree_factor": gaussian(key_list[0], (LAYERS, SUB, NS, NB, NS * NB), (2 * NS * NB) ** -0.5, 0.09375, ((0, 2), (3, 4), (4, 4)), jnp.float32),
        "sub_linv": draw_sub_linv(jax.random.fold_in(key_list[11], 71), 0),
        "sub_uinv": draw_sub_uinv(jax.random.fold_in(key_list[11], 71), 0),
        "lower_panel": gaussian(key_list[3], (LAYERS, NT, NB, SUB, NS * NB), (2 * LAYERS * SUB * NS * NB) ** -0.5, 0.046875, ((0, 2), (2, 4), (4, 4)), jnp.float32),
        "upper_panel": gaussian(key_list[4], (LAYERS, SUB, NS, NB, NT * NB), (2 * NT * NB) ** -0.5, 0.125, ((0, 2), (3, 4), (4, 4)), jnp.float32),
        "panel_rows": touch_ends((jax.random.randint(key_list[5], (LAYERS, NT, SUB), 0, 3) < 2).astype(jnp.int32), jax.random.fold_in(key_list[5], 1), 0, 1),
        "upper_level_factor": gaussian(key_list[6], (NT, NB, NT * NB), (2 * NT * NB) ** -0.5, 0.125, ((1, 4), (2, 4)), jnp.float32),
        "top_linv": draw_top_linv(jax.random.fold_in(key_list[11], 71), 0),
        "top_uinv": draw_top_uinv(jax.random.fold_in(key_list[11], 71), 0),
        "sub_rhs": gaussian(key_list[9], (LAYERS, SUB, NS, NB, NR), 1.0, 6.0, ((0, 2), (3, 4)), jnp.float32),
        "top_rhs": gaussian(key_list[10], (NT, NB, NR), 1.0, 6.0, ((1, 4), (2, 2)), jnp.float32),
    }


TOP_PRECISION = lax.Precision.HIGHEST


def solve_chain(blocks, inverses, right_side, coupling, forward):
    block_count = blocks.shape[2]
    solved = jnp.zeros(right_side.shape, jnp.float32)
    order_list = range(block_count) if forward else range(block_count - 1, -1, -1)
    for sweep_step_index in order_list:
        first_block, last_block = (0, sweep_step_index) if forward else (sweep_step_index + 1, block_count)
        partial_value = coupling[:, :, sweep_step_index]
        if last_block > first_block:
            partial_value = partial_value + jnp.einsum('jsakb,jskbr->jsar', blocks[:, :, sweep_step_index, :, first_block:last_block], solved[:, :, first_block:last_block], precision=TOP_PRECISION)
        block_value = jnp.einsum('jsab,jsar->jsbr', inverses[:, :, sweep_step_index], right_side[:, :, sweep_step_index] - partial_value, precision=TOP_PRECISION)
        solved = solved.at[:, :, sweep_step_index].set(block_value)
    return solved


def reference(subtree_factor, sub_linv, sub_uinv, lower_panel, upper_panel, panel_rows, upper_level_factor, top_linv, top_uinv, sub_rhs, top_rhs):
    layers, groups, block_count, block_rows, columns = sub_rhs.shape
    top_count = top_rhs.shape[0]
    sub_blocks = subtree_factor.reshape(layers, groups, block_count, block_rows, block_count, block_rows)
    top_blocks = upper_level_factor.reshape(1, 1, top_count, block_rows, top_count, block_rows)
    present = panel_rows.astype(jnp.float32)
    lower_sub = solve_chain(sub_blocks, sub_linv, sub_rhs, jnp.zeros(sub_rhs.shape, jnp.float32), True)

    def add_layer(carried, pieces):
        panel_piece, mask_piece, solved_piece = pieces
        flat_solved = solved_piece.reshape(groups, block_count * block_rows, columns)
        layer_term = jnp.einsum('tasm,ts,smr->tar', panel_piece, mask_piece, flat_solved, precision=TOP_PRECISION)
        return carried + layer_term, None

    contrib, ignored = lax.scan(add_layer, jnp.zeros(top_rhs.shape, jnp.float32), (lower_panel, present, lower_sub))
    upper_level_lower = solve_chain(top_blocks, top_linv[None, None], top_rhs[None, None], contrib[None, None], True)
    top_solution = solve_chain(top_blocks, top_uinv[None, None], upper_level_lower, jnp.zeros(upper_level_lower.shape, jnp.float32), False)[0, 0]
    upper_blocks = upper_panel.reshape(layers, groups, block_count, block_rows, top_count, block_rows)
    coupling = jnp.einsum('jskatb,jts,tbr->jskar', upper_blocks, present, top_solution, precision=TOP_PRECISION)
    sub_solution = solve_chain(sub_blocks, sub_uinv, lower_sub, coupling, False)
    return sub_solution, top_solution
```

```python
import jax
import jax.numpy as jnp
from jax import lax
from jax.sharding import PartitionSpec as P

PRECISION = lax.Precision.HIGHEST


def mul(a, b):
    return jnp.dot(a, b, precision=PRECISION, preferred_element_type=jnp.float32)


def mul_t(a, b):
    return lax.dot_general(
        a, b, (((0,), (0,)), ((), ())), precision=PRECISION, preferred_element_type=jnp.float32
    )


def pick(stack, index):
    return lax.dynamic_index_in_dim(stack, index, 0, keepdims=False)


class Grid:
    def __init__(self, groups, columns):
        self.nz = lax.axis_size("prow")
        self.nc = lax.axis_size("pcol")
        self.nl = lax.axis_size("leaf")
        self.groups = groups
        self.parts = self.nc // groups
        self.columns = columns // self.parts
        self.z = lax.axis_index("prow")
        self.c = lax.axis_index("pcol")
        self.l = lax.axis_index("leaf")
        self.s = self.c // self.parts
        self.h = self.c % self.parts

    def from_z(self, x, d):
        return lax.ppermute(x, "prow", [((i + d) % self.nz, i) for i in range(self.nz)])

    def from_l(self, x, d):
        return lax.ppermute(x, "leaf", [((i + d) % self.nl, i) for i in range(self.nl)])

    def from_c(self, x, ds, dh):
        g, k = self.groups, self.parts
        return lax.ppermute(
            x,
            "pcol",
            [
                (((i // k + ds) % g) * k + (i % k + dh) % k, i)
                for i in range(self.nc)
            ],
        )

    def gather_z(self, x):
        return [x] + [self.from_z(x, d) for d in range(1, self.nz)]

    def gather_h(self, x):
        stack = jnp.stack([x] + [self.from_c(x, 0, d) for d in range(1, self.parts)])
        return [pick(stack, (q - self.h) % self.parts) for q in range(self.parts)]

    def natural_c(self, rel):
        stack = jnp.stack([b for row in rel for b in row])
        out = []
        for p in range(self.nc):
            ds = (p // self.parts - self.s) % self.groups
            dh = (p % self.parts - self.h) % self.parts
            out.append(pick(stack, ds * self.parts + dh))
        return out

    def columns_of(self, per_group):
        rows = [pick(per_group, self.s)]
        for d in range(1, self.groups):
            rows.append(self.from_c(pick(per_group, (self.s - d) % self.groups), d, 0))
        mine = jnp.stack(rows)
        rel = [[rows[d]] for d in range(self.groups)]
        for e in range(1, self.parts):
            got = self.from_c(mine, 0, e)
            for d in range(self.groups):
                rel[d].append(got[d])
        return self.natural_c(rel)

    def all_columns(self, x):
        rel = [[x] + [None] * (self.parts - 1) for _ in range(self.groups)]
        rows = [x] + [self.from_c(x, d, 0) for d in range(1, self.groups)]
        mine = jnp.stack(rows)
        rel = [[r] for r in rows]
        for e in range(1, self.parts):
            got = self.from_c(mine, 0, e)
            for d in range(self.groups):
                rel[d].append(got[d])
        return self.natural_c(rel)


def group_bulk(grid, inverses, factor, rows, forward, nb):
    pieces, widths = [], []
    for n, i in enumerate(rows):
        first = min(rows[0], i + 1) if not forward else rows[0]
        lo, hi = (rows[0], i) if forward else (i + 1, rows[0] + 1)
        pieces.append(inverses[i])
        widths.append(nb)
        if hi > lo:
            pieces.append(factor[i][:, lo * nb : hi * nb])
            widths.append((hi - lo) * nb)
    tile = jnp.concatenate(pieces, axis=1)
    part = tile.shape[1] // grid.parts
    mine = lax.dynamic_slice_in_dim(tile, grid.h * part, part, 1)
    whole = jnp.concatenate(grid.gather_z(mine), axis=0)
    whole = jnp.concatenate(grid.gather_h(whole), axis=1)
    out, at = [], 0
    for w in widths:
        out.append(whole[:, at : at + w])
        at += w
    return out


def solve_group(bulk, right, rows, forward):
    solved, at = [], 0
    for n in range(len(rows)):
        inverse = bulk[at]
        at += 1
        side = right[n]
        if n:
            known = solved if forward else solved[::-1]
            side = side - mul(bulk[at], jnp.concatenate(known, axis=0))
            at += 1
        solved.append(mul_t(inverse, side))
    return solved


def sweep(grid, groups, bulks, factor, tiles, forward, nb, extra=None):
    tiles = list(tiles)
    count = len(tiles)
    solved = [None] * count
    total = None
    tile_rows = tiles[0].shape[0]
    for g, rows in enumerate(groups):
        sent = jnp.concatenate([tiles[i] for i in rows], axis=0)
        got = grid.gather_z(sent)
        right = [
            jnp.concatenate([t[n * tile_rows : (n + 1) * tile_rows] for t in got], axis=0)
            for n in range(len(rows))
        ]
        out = solve_group(bulks[g], right, rows, forward)
        for i, x in zip(rows, out):
            solved[i] = x
        lo, hi = min(rows), max(rows) + 1
        block = jnp.concatenate([solved[i] for i in range(lo, hi)], axis=0)
        left = [i for later in groups[g + 1 :] for i in later]
        for later in ([groups[g + 1]] if g + 1 < len(groups) else []) + [
            [i for more in groups[g + 2 :] for i in more]
        ]:
            if not later:
                continue
            a = jnp.concatenate([factor[i][:, lo * nb : hi * nb] for i in later], axis=0)
            change = mul(a, block)
            for n, i in enumerate(later):
                tiles[i] = tiles[i] - change[n * tile_rows : (n + 1) * tile_rows]
        if extra is not None:
            term = mul(extra[:, lo * nb : hi * nb], block)
            total = term if total is None else total + term
    return solved, total


def chunks(count, size, forward):
    order = list(range(count)) if forward else list(range(count - 1, -1, -1))
    return [order[i : i + size] for i in range(0, count, size)]


def per_device(
    subtree_factor,
    sub_linv,
    sub_uinv,
    lower_panel,
    upper_panel,
    panel_rows,
    upper_level_factor,
    top_linv,
    top_uinv,
    sub_rhs,
    top_rhs,
):
    _, groups, count, tile_rows, nrhs = sub_rhs.shape
    nb = sub_linv.shape[4]
    nt = top_rhs.shape[0]
    grid = Grid(groups, nrhs)
    owned = subtree_factor.shape[4] // nb
    top_owned = upper_level_factor.shape[2] // nb
    present = lax.dynamic_index_in_dim(
        panel_rows[0].astype(jnp.float32), grid.s, 1, keepdims=False
    )

    def own_columns(x):
        return lax.dynamic_slice_in_dim(x, grid.h * grid.columns, grid.columns, x.ndim - 1)

    linv = pick(sub_linv[0], grid.s)
    uinv = pick(sub_uinv[0], grid.s)
    factor = []
    for q in range(0, count, owned):
        cols = grid.columns_of(subtree_factor[0][:, q : q + owned])
        for i in range(owned):
            factor.append(jnp.concatenate([b[i] for b in cols], axis=1))
    forward_groups = chunks(count, 2, True)
    backward_groups = chunks(count, 2, False)
    forward_bulks = [group_bulk(grid, linv, factor, g, True, nb) for g in forward_groups]
    panel = lower_panel[0].transpose(2, 0, 1, 3)
    panel = jnp.concatenate(grid.columns_of(panel), axis=2)
    panel = panel.reshape(nt * tile_rows, count * nb)

    rhs = own_columns(pick(sub_rhs[0], grid.s))
    lower, contrib = sweep(
        grid, forward_groups, forward_bulks, factor, rhs, True, nb, extra=panel
    )

    both = jnp.concatenate([top_linv, top_uinv], axis=2)
    part = both.shape[2] // grid.nc
    both = lax.dynamic_slice_in_dim(both, grid.c * part, part, 2)
    top_tile = jnp.concatenate([upper_level_factor, both], axis=2)
    top_mine = jnp.stack(grid.gather_z(top_tile), axis=1)
    top_mine = top_mine.reshape(nt, grid.nz * tile_rows, top_tile.shape[2])
    top_all = grid.all_columns(top_mine)
    wide = upper_level_factor.shape[2]
    top_factor = jnp.concatenate([b[:, :, :wide] for b in top_all], axis=2)
    top_both = jnp.concatenate([b[:, :, wide:] for b in top_all], axis=2)
    sides = jnp.stack([top_rhs] + [grid.from_l(top_rhs, d) for d in range(1, grid.nl)])
    side = jnp.concatenate([pick(sides, (q - grid.l) % grid.nl) for q in range(grid.nl)], axis=2)
    side = own_columns(side)

    contrib = contrib.reshape(nt, tile_rows, grid.columns) * present[:, None, None]
    if grid.nl * groups <= 4:
        total = contrib
        for dl in range(grid.nl):
            for ds in range(groups):
                if dl or ds:
                    pairs = [
                        (
                            ((j + dl) % grid.nl) * grid.nc
                            + ((c // grid.parts + ds) % groups) * grid.parts
                            + c % grid.parts,
                            j * grid.nc + c,
                        )
                        for j in range(grid.nl)
                        for c in range(grid.nc)
                    ]
                    total = total + lax.ppermute(contrib, ("leaf", "pcol"), pairs)
    else:
        total = contrib
        for ds in range(1, groups):
            total = total + grid.from_c(contrib, ds, 0)
        total = lax.psum(total, "leaf")
    got = grid.gather_z((side - total).reshape(nt * tile_rows, grid.columns))
    right = [
        jnp.concatenate([g[t * tile_rows : (t + 1) * tile_rows] for g in got], axis=0)
        for t in range(nt)
    ]
    top_lower = []
    for t in range(nt):
        r = right[t]
        if t:
            r = r - mul(top_factor[t][:, : t * nb], jnp.concatenate(top_lower, axis=0))
        top_lower.append(mul_t(top_both[t][:, :nb], r))
    top_x = [None] * nt
    for t in range(nt - 1, -1, -1):
        r = jnp.concatenate([top_lower[t], top_lower[t]], axis=0)
        r = lax.dynamic_slice_in_dim(r, grid.z * tile_rows, nb, 0)
        if t < nt - 1:
            r = r - mul(top_factor[t][:, (t + 1) * nb :], jnp.concatenate(top_x[t + 1 :], axis=0))
        top_x[t] = mul_t(top_both[t][:, nb:], r)
    top_stack = jnp.stack(top_x)

    def top_of(c):
        return lax.dynamic_slice_in_dim(top_stack, c * top_owned, top_owned, 0)

    outs = [top_of(grid.c)]
    for e in range(1, grid.parts):
        dest = grid.s * grid.parts + (grid.h - e) % grid.parts
        outs.append(grid.from_c(top_of(dest), 0, e))
    outs = jnp.stack(outs)
    top_out = jnp.concatenate(
        [pick(outs, (q - grid.h) % grid.parts) for q in range(grid.parts)], axis=2
    )
    top_out = lax.dynamic_slice_in_dim(top_out, grid.l * top_rhs.shape[2], top_rhs.shape[2], 2)

    upper = grid.columns_of(upper_panel[0])
    upper = jnp.concatenate(upper, axis=2).reshape(count * tile_rows, nt * nb)
    masked = (top_stack * present[:, None, None]).reshape(nt * nb, grid.columns)
    coupling = mul(upper, masked).reshape(count, tile_rows, grid.columns)
    backward_bulks = [group_bulk(grid, uinv, factor, g, False, nb) for g in backward_groups]
    tiles = [
        lax.dynamic_slice_in_dim(lower[i], grid.z * tile_rows, tile_rows, 0) - coupling[i]
        for i in range(count)
    ]
    solved, _ = sweep(grid, backward_groups, backward_bulks, factor, tiles, False, nb)
    stack = jnp.stack(solved)

    def pair_of(c):
        return lax.dynamic_slice_in_dim(stack, c * owned, owned, 0)

    rel = []
    for ds in range(groups):
        for dh in range(grid.parts):
            if ds == 0 and dh == 0:
                rel.append(pair_of(grid.c))
                continue
            dest = ((grid.s - ds) % groups) * grid.parts + (grid.h - dh) % grid.parts
            rel.append(grid.from_c(pair_of(dest), ds, dh))
    rel = jnp.stack(rel)
    out = []
    for sg in range(groups):
        row = []
        for q in range(grid.parts):
            index = ((sg - grid.s) % groups) * grid.parts + (q - grid.h) % grid.parts
            row.append(pick(rel, index))
        out.append(jnp.concatenate(row, axis=2))
    return (jnp.stack(out)[None], top_out)


def solution(mesh):
    placed = (
        P("leaf", None, None, "prow", "pcol"),
        P("leaf", None, None, "prow", None),
        P("leaf", None, None, "prow", None),
        P("leaf", None, "prow", None, "pcol"),
        P("leaf", None, None, "prow", "pcol"),
        P("leaf", None, None),
        P(None, "prow", "pcol"),
        P(None, "prow", None),
        P(None, "prow", None),
        P("leaf", None, None, "prow", None),
        P(None, "prow", "leaf"),
    )
    return jax.shard_map(
        per_device,
        mesh=mesh,
        in_specs=placed,
        out_specs=(P("leaf", None, "pcol", None, None), P("pcol", None, "leaf")),
        check_vma=False,
    )
```

```python
import functools

import jax
import jax.numpy as jnp
from jax import lax
from jax.experimental import pallas as pl
from jax.experimental.pallas import tpu as pltpu
from jax.sharding import PartitionSpec as P

PRECISION = lax.Precision.HIGHEST
VMEM = pl.BlockSpec(memory_space=pltpu.VMEM)
LEFT = pl.BlockSpec(memory_space=pltpu.VMEM)
SMEM = pl.BlockSpec(memory_space=pltpu.SMEM)
ANY = pl.BlockSpec(memory_space=pltpu.HBM)
ARG = pl.BlockSpec(memory_space=pltpu.HBM)
F32 = jnp.float32
GRANT = 16 * 1024 * 1024


def dot(a, b):
    return lax.dot_general(
        a, b, (((1,), (0,)), ((), ())), precision=PRECISION, preferred_element_type=F32
    )


def dot_t(a, b):
    return lax.dot_general(
        a, b, (((0,), (0,)), ((), ())), precision=PRECISION, preferred_element_type=F32
    )


def shaped(*shape):
    return jax.ShapeDtypeStruct(shape, F32)


def after(x, dep):
    return x if dep is None else lax.optimization_barrier((x, dep))[0]


def pick(stack, index):
    return lax.dynamic_index_in_dim(stack, index, 0, keepdims=False)


class Grid:
    def __init__(self, groups, columns):
        self.nz = lax.axis_size("prow")
        self.nc = lax.axis_size("pcol")
        self.nl = lax.axis_size("leaf")
        self.groups = groups
        self.parts = self.nc // groups
        self.columns = columns // self.parts
        self.moves = [
            (ds, dh) for ds in range(groups) for dh in range(self.parts)
        ]

    @property
    def z(self):
        return lax.axis_index("prow")

    @property
    def c(self):
        return lax.axis_index("pcol")

    @property
    def l(self):
        return lax.axis_index("leaf")

    @property
    def s(self):
        return lax.div(self.c, jnp.int32(self.parts))

    @property
    def h(self):
        return lax.rem(self.c, jnp.int32(self.parts))

    def block(self, ds, dh):
        return lax.rem(self.s + ds, jnp.int32(self.groups)) * self.parts + self.part(dh)

    def part(self, dh):
        return lax.rem(self.h + dh, jnp.int32(self.parts))

    def row(self, d):
        return lax.rem(self.z + d, jnp.int32(self.nz))

    def from_z(self, x, d):
        return lax.ppermute(x, "prow", [((i + d) % self.nz, i) for i in range(self.nz)])

    def from_l(self, x, d):
        return lax.ppermute(x, "leaf", [((i + d) % self.nl, i) for i in range(self.nl)])

    def from_c(self, x, ds, dh):
        g, k = self.groups, self.parts
        return lax.ppermute(
            x,
            "pcol",
            [(((i // k + ds) % g) * k + (i % k + dh) % k, i) for i in range(self.nc)],
        )

    def gather_z(self, x):
        return [x] + [self.from_z(x, d) for d in range(1, self.nz)]


def call(body, ins, specs, outs, out_specs, scratch, name, us):
    ins = [
        pltpu.with_memory_space_constraint(x, pltpu.HBM) if spec in (ANY, ARG) else x
        for x, spec in zip(ins, specs)
    ]
    return pl.pallas_call(
        body,
        out_shape=tuple(
            pltpu.VMEM(o.shape, o.dtype) if spec is VMEM else o for o, spec in zip(outs, out_specs)
        ),
        in_specs=list(specs),
        out_specs=tuple(out_specs),
        scratch_shapes=list(scratch),
        compiler_params=pltpu.CompilerParams(vmem_limit_bytes=GRANT),
        cost_estimate=pl.CostEstimate(
            flops=int(us * 1.1e9), bytes_accessed=int(us * 3.6e6), transcendentals=0
        ),
        name=name,
    )(*ins)


def start_all(jobs, sem):
    for n, (cond, src, dst) in enumerate(jobs):
        copy = pltpu.make_async_copy(src, dst, sem.at[n])
        if cond is None:
            copy.start()
        else:
            pl.when(cond)(copy.start)


def wait_all(jobs, sem):
    for n, (cond, src, dst) in enumerate(jobs):
        copy = pltpu.make_async_copy(src, dst, sem.at[n])
        if cond is None:
            copy.wait()
        else:
            pl.when(cond)(copy.wait)


def move(ins, outs, plan, many, name, final=False, args=0):
    def body(*refs):
        sem = refs[-1]
        jobs = plan(refs[: len(ins)], refs[len(ins) : -1])
        start_all(jobs, sem)
        wait_all(jobs, sem)

    return call(
        body,
        ins,
        [ARG] * args + [ANY] * (len(ins) - args),
        outs,
        [LEFT if final else VMEM] * len(outs),
        [pltpu.SemaphoreType.DMA((many,))],
        name,
        1,
    )


def per_device(
    subtree_factor,
    sub_linv,
    sub_uinv,
    lower_panel,
    upper_panel,
    panel_rows,
    upper_level_factor,
    top_linv,
    top_uinv,
    sub_rhs,
    top_rhs,
):
    _, groups, count, rows, nrhs = sub_rhs.shape
    nb = sub_linv.shape[4]
    nt = top_rhs.shape[0]
    grid = Grid(groups, nrhs)
    nz, nc, nl, parts, cols = grid.nz, grid.nc, grid.nl, grid.parts, grid.columns
    owned = subtree_factor.shape[4] // nb
    top_owned = upper_level_factor.shape[2] // nb
    part = nb // parts
    wide = owned * nb
    early = count // 2
    share = nt * rows // nl
    piece = min(share, rows)
    top_wide = upper_level_factor.shape[2]
    top_pieces = top_wide // part
    cut = (count - early) * rows
    factor, linv, uinv = subtree_factor[0], sub_linv[0], sub_uinv[0]
    rhs = sub_rhs[0]

    def own_part(width):
        return pl.ds(pl.multiple_of(grid.h * width, width), width)

    def rows_at(d):
        return pl.ds(pl.multiple_of(grid.row(d) * rows, rows), rows)

    order = list(range(1, count)) + [0]
    chunks = [order[:owned], order[owned : 2 * owned], order[2 * owned :]]
    where = {i: (n, k) for n, chunk in enumerate(chunks) for k, i in enumerate(chunk)}

    def other(ds):
        return lax.rem(grid.s + (groups - ds), jnp.int32(groups))

    def plan_first(ins, outs):
        rhs_, linv_, factor_ = ins
        m0 = outs[0]
        jobs = [
            (None, rhs_.at[grid.s, 0, :, own_part(cols)], m0.at[:, pl.ds(0, cols)]),
            (None, linv_.at[grid.s, 0], m0.at[:, pl.ds(cols, nb)]),
        ]
        for i in range(1, early):
            at = pl.ds(cols + nb + (i - 1) * part, part)
            jobs.append((None, linv_.at[grid.s, i, :, own_part(part)], m0.at[:, at]))
        for ds in range(1, groups):
            for k, i in enumerate(chunks[0]):
                jobs.append((None, factor_.at[other(ds), i], outs[ds].at[k]))
        return jobs

    first = move(
        [rhs, linv, factor],
        [shaped(rows, cols + nb + (early - 1) * part)]
        + [shaped(owned, rows, wide)] * (groups - 1),
        plan_first,
        1 + early + (groups - 1) * owned,
        "pack_first",
        args=3,
    )
    m0 = grid.gather_z(first[0])
    y_got, sources = {}, {}
    for ds in range(1, groups):
        y_got[ds, 0] = grid.from_c(first[ds], ds, 0)

    def plan_second(ins, outs):
        jobs = [(None, ins[0].at[grid.s], outs[0])]
        for ds in range(1, groups):
            for n in range(1, len(chunks)):
                target = outs[(ds - 1) * (len(chunks) - 1) + n]
                for k, i in enumerate(chunks[n]):
                    jobs.append((None, ins[0].at[other(ds), i], target.at[k]))
        return jobs

    second = move(
        [after(factor, first[0])],
        [shaped(count, rows, wide)]
        + [shaped(len(chunk), rows, wide) for chunk in chunks[1:]] * (groups - 1),
        plan_second,
        1 + count * groups,
        "pack_second",
        args=1,
    )
    own = second[0]

    def plan_core(ins, outs):
        jobs = [(None, ins[0].at[chunks[0][0]], outs[0].at[0])]
        for ds in range(1, groups):
            jobs.append((None, ins[ds], outs[0].at[pl.ds(1 + (ds - 1) * owned, owned)]))
        return jobs

    (core,) = move(
        [own] + after([y_got[ds, 0] for ds in range(1, groups)], m0),
        [shaped(1 + (groups - 1) * owned, rows, wide)],
        plan_core,
        groups,
        "pack_core",
    )
    cores = {dh: grid.from_c(core, 0, dh) for dh in range(1, parts)}

    def start_chunk(n, dep):
        for ds in range(1, groups):
            sent = second[(ds - 1) * (len(chunks) - 1) + n]
            y_got[ds, n] = grid.from_c(after(sent, dep), ds, 0)
        return [y_got[ds, n] for ds in range(1, groups)]

    def share_chunk(n, dep):
        for ds in range(1, groups):
            for dh in range(1, parts):
                y_got[ds, dh, n] = grid.from_c(after(y_got[ds, n], dep), 0, dh)

    def row_sources(i):
        n, k = where[i]
        out = []
        for ds, dh in grid.moves:
            if dh == 0:
                out.append((y_got[ds, n], k) if ds else (own, i))
            elif n == 0 and ds:
                out.append((cores[dh], 1 + (ds - 1) * owned + k))
            elif ds:
                out.append((y_got[ds, dh, n], k))
            else:
                out.append((cores[dh], 0) if i == chunks[0][0] else (sources[0, dh], i))
        return out

    def plan_bulk(ins, outs):
        linv_, top_, tl_, tu_ = ins
        bulk = outs[0]
        jobs = []
        for k in range(count - early):
            jobs.append(
                (
                    None,
                    linv_.at[grid.s, early + k, :, own_part(part)],
                    bulk.at[pl.ds(k * rows, rows)],
                )
            )
        for a in range(share // piece):
            flat = grid.l * share + a * piece
            t = lax.div(flat, jnp.int32(rows))
            at = pl.ds(pl.multiple_of(lax.rem(flat, jnp.int32(rows)), piece), piece)
            for n in range(top_pieces + 1):
                target = bulk.at[pl.ds(cut + n * share + a * piece, piece)]
                if n < top_pieces:
                    jobs.append((None, top_.at[t, at, pl.ds(n * part, part)], target))
                    continue
                half = nb // part
                low = pl.ds(pl.multiple_of(lax.rem(grid.c, jnp.int32(half)) * part, part), part)
                jobs.append((grid.c < half, tl_.at[t, at, low], target))
                jobs.append((grid.c >= half, tu_.at[t, at, low], target))
        return jobs

    (bulk,) = move(
        [after(linv, m0), upper_level_factor, top_linv, top_uinv],
        [shaped(cut + (top_pieces + 1) * share, part)],
        plan_bulk,
        count - early + (top_pieces + 2) * (share // piece),
        "pack_bulk",
        args=4,
    )
    gathered = lax.all_gather(bulk, "prow")

    def place_early(tiles, many, at):
        def plan(ins, outs):
            return [
                (None, ins[d].at[:, pl.ds(at + k * part, part)], outs[0].at[k, rows_at(d)])
                for d in range(nz)
                for k in range(many)
            ]

        (mine,) = move(
            tiles, [shaped(many, nz * rows, part)], plan, nz * many, "place_early"
        )
        return [mine] + [grid.from_c(mine, 0, dh) for dh in range(1, parts)]

    early_inv = []

    def plan_late(ins, outs):
        jobs = [
            (
                None,
                ins[0].at[a, pl.ds(k * rows, rows)],
                outs[0].at[k, pl.ds(a * rows, rows)],
            )
            for a in range(nz)
            for k in range(count - early)
        ]
        size = (top_pieces + 1) * share
        return jobs + [(None, ins[0].at[:, pl.ds(cut, size)], outs[1])]

    late_inv = []

    def place_late(dep):
        mine, top_mine = move(
            [after(gathered, dep)],
            [
                shaped(count - early, nz * rows, part),
                shaped(nz, (top_pieces + 1) * share, part),
            ],
            plan_late,
            nz * (count - early) + 1,
            "place_late",
        )
        late_inv.extend([mine] + [grid.from_c(mine, 0, dh) for dh in range(1, parts)])
        return top_mine

    def inverse_of(i):
        if i < early:
            return early_inv, i - 1
        return late_inv, i - early

    def fetch(i, refs, scratch, slot):
        return [
            (None, ref.at[index], scratch.at[slot, grid.block(ds, dh)])
            for (ds, dh), ref, (_, index) in zip(grid.moves, refs, row_sources(i))
        ]

    def solved_sum(acc, scratch, slot, known):
        for k, x in known:
            acc = acc - dot(
                scratch[slot, k // owned, :, (k % owned) * nb : (k % owned + 1) * nb], x[...]
            )
        return acc

    nsrc = len(grid.moves)

    def forward_step(i, pieces, solved, extra=()):
        last = i == count - 1
        ins, specs = list(pieces), [VMEM] * nz
        if i:
            stack, index = inverse_of(i)
            ins += stack
            specs += [ANY] * parts
        ninv = len(ins) - nz
        ins += solved
        specs += [VMEM] * len(solved)
        if last:
            ins += list(extra)
            specs += [VMEM, VMEM, SMEM]
        else:
            ins += [a for a, _ in row_sources(i + 1)] + [rhs]
            specs += [ANY] * nsrc + [ARG]

        def body(*refs):
            got = refs[:nz]
            inv = refs[nz : nz + ninv]
            known = refs[nz + ninv : nz + ninv + len(solved)]
            rest = refs[nz + ninv + len(solved) : len(ins)]
            x_ref, next_ref = refs[len(ins) : len(ins) + 2]
            r_scr, i_scr, f_scr, t_scr, sem, i_sem = refs[len(ins) + 2 :]
            inv_jobs = [
                (None, inv[e].at[index], i_scr.at[:, pl.ds(e * part, part)]) for e in range(ninv)
            ]
            start_all(inv_jobs, i_sem)
            if not last:
                jobs = fetch(i + 1, rest[:nsrc], f_scr, 0)
                jobs.append((None, rest[nsrc].at[grid.s, i + 1, :, own_part(cols)], t_scr))
                start_all(jobs, sem)
            for d in range(nz):
                r_scr[rows_at(d)] = got[d][:, :cols]
                if i == 0:
                    i_scr[rows_at(d)] = got[d][:, cols : cols + nb]
            if i == 0:
                x_ref[...] = dot_t(i_scr[...], r_scr[...])
            wait_all(inv_jobs, i_sem)
            for e in range(ninv):
                at = pl.ds(pl.multiple_of(grid.part(e) * part, part), part)
                x_ref[at] = dot_t(i_scr[:, e * part : (e + 1) * part], r_scr[...])
            if last:
                total = rest[0][...] + dot(rest[1][...], x_ref[...])
                for t in range(nt):
                    at = slice(t * rows, (t + 1) * rows)
                    next_ref[at] = total[at] * rest[2][t]
            else:
                wait_all(jobs, sem)
                known = list(enumerate(known)) + [(i, x_ref)]
                next_ref[...] = solved_sum(t_scr[...], f_scr, 0, known)

        return call(
            body,
            ins,
            specs,
            [shaped(nb, cols), shaped(nt * rows if last else rows, cols)],
            [VMEM, VMEM],
            [
                pltpu.VMEM((nz * rows, cols), F32),
                pltpu.VMEM((nz * rows, nb), F32),
                pltpu.VMEM((1, nc, rows, wide), F32),
                pltpu.VMEM((rows, cols), F32),
                pltpu.SemaphoreType.DMA((nsrc + 1,)),
                pltpu.SemaphoreType.DMA((parts,)),
            ],
            "forward_step",
            4,
        )

    present = lax.dynamic_index_in_dim(panel_rows[0].astype(F32), grid.s, 1, keepdims=False)
    per = owned * (owned + 1) // 2
    def plan_back(ins, outs):
        out = outs[0]
        jobs = []
        for p in range(nc):
            base = (nc - 1 - p) * per * part
            for n in range(owned):
                jobs.append(
                    (
                        None,
                        ins[0].at[grid.s, p * owned + owned - 1 - n, :, own_part(part)],
                        out.at[:, pl.ds(base + n * part, part)],
                    )
                )
        at = 1
        for ds, dh in grid.moves:
            p = grid.block(ds, dh)
            col = pl.ds(pl.multiple_of(nb + grid.h * part, part), part)
            to = pl.ds(pl.multiple_of((nc - 1 - p) * per * part + owned * part, part), part)
            if ds == 0:
                jobs.append((None, ins[at].at[p * owned, :, col], out.at[:, to]))
                at += 1
                continue
            for q in range(nc):
                n, k = where[q * owned]
                if dh and not n:
                    k += 1 + (ds - 1) * owned
                jobs.append((p == q, ins[at + n].at[k, :, col], out.at[:, to]))
            at += len(chunks)
        return jobs

    def pack_back():
        ins = [after(uinv, lower[2])]
        for ds, dh in grid.moves:
            if ds == 0:
                ins.append(own if dh == 0 else sources[0, dh])
            else:
                for n in range(len(chunks)):
                    if dh == 0:
                        ins.append(y_got[ds, n])
                    else:
                        ins.append(y_got[ds, dh, n] if n else cores[dh])
        (back,) = move(
            ins, [shaped(rows, nc * per * part)], plan_back, nc * owned + nsrc * nc, "pack_back", args=1
        )
        return back

    def top_side(dep):
        mine = after(top_rhs, dep)
        sides = jnp.stack([mine] + [grid.from_l(mine, d) for d in range(1, nl)])
        side = jnp.concatenate([pick(sides, (q - grid.l) % nl) for q in range(nl)], axis=2)
        side = lax.dynamic_slice_in_dim(side, grid.h * cols, cols, 2)
        return side.reshape(nt * rows, cols)

    lower = []
    lp, top_got = {}, {}
    panel = lower_panel[0]

    def panel_of(s, dep):
        x = lax.dynamic_index_in_dim(panel, after(s, dep), 2, keepdims=False)
        return x.reshape(nt * rows, wide)

    pieces = m0
    for i in range(count):
        due = []
        if i == 1:
            early_inv.extend(place_early(after(m0, lower[0]), early - 1, cols + nb))
            for dh in range(1, parts):
                sources[0, dh] = grid.from_c(after(own, lower[0]), 0, dh)
            due += start_chunk(1, lower[0])
        if i == 2:
            share_chunk(1, lower[1])
            in_flight = start_chunk(2, lower[1])
        if i == early - 1:
            due += in_flight
            share_chunk(2, lower[-1])
            top_mine = place_late((lower[-1], pieces))
            top_got[0, 0] = top_mine
        if i == early:
            held = (lower[-1], late_inv)
            for dl in range(1, nl):
                top_got[dl, 0] = grid.from_l(after(top_mine, held), dl)
            for ds in range(1, groups):
                top_got[0, ds] = grid.from_c(after(top_mine, held), ds, 0)
        if i == early - 2:
            side = top_side(lower[-1])
        if i == early - 1:
            due.append(side)
        if i == early + 1:
            back = pack_back()
            due.append(back)
            back = lax.all_gather(back, "prow")
            due += [top_got[k] for k in top_got if any(k)]
        if i == 7:
            due.append(back)
        if i == early + 2:
            for ds in range(1, groups):
                for dl in range(1, nl):
                    top_got[dl, ds] = grid.from_l(after(top_got[0, ds], lower[-1]), dl)
            lp[0, 0] = panel_of(grid.s, lower[2])
            for ds in range(1, groups):
                lp[ds, 0] = grid.from_c(after(panel_of(other(ds), lower[2]), lower[-1]), ds, 0)
                due.append(lp[ds, 0])
        pieces = after(pieces, due)
        if i == count - 1:
            def panel_body(*refs):
                srcs, known = refs[:nsrc], refs[nsrc : nsrc + count - 1]
                total, block, scr, sem = refs[nsrc + count - 1 :]
                jobs = [
                    (None, ref, scr.at[grid.block(ds, dh)])
                    for (ds, dh), ref in zip(grid.moves, srcs)
                ]
                start_all(jobs, sem)
                wait_all(jobs, sem)
                acc = None
                for k, x in enumerate(known):
                    a = scr[k // owned, :, (k % owned) * nb : (k % owned + 1) * nb]
                    term = dot(a, x[...])
                    acc = term if acc is None else acc + term
                total[...] = acc
                block[...] = scr[nc - 1, :, (owned - 1) * nb :]

            for ds in range(groups):
                for dh in range(1, parts):
                    lp[ds, dh] = grid.from_c(after(lp[ds, 0], lower[-1]), 0, dh)
            total, block = call(
                panel_body,
                [lp[m] for m in grid.moves] + lower,
                [ANY] * nsrc + [VMEM] * (count - 1),
                [shaped(nt * rows, cols), shaped(nt * rows, nb)],
                [VMEM, VMEM],
                [pltpu.VMEM((nc, nt * rows, wide), F32), pltpu.SemaphoreType.DMA((nsrc,))],
                "panel_sums",
                3,
            )
            x, contrib = forward_step(i, pieces, lower, (total, block, present))
        else:
            x, sent = forward_step(i, pieces, lower)
            pieces = grid.gather_z(sent)
        lower.append(x)


    keys = sorted(top_got)
    group_wide = top_wide + part

    def plan_top(ins, outs):
        jobs = []
        for (dl, ds), ref in zip(keys, ins):
            base = lax.rem(grid.s + ds, jnp.int32(groups)) * group_wide
            flat = lax.rem(grid.l + dl, jnp.int32(nl)) * share
            for a in range(share // piece):
                at = flat + a * piece
                t = lax.div(at, jnp.int32(rows))
                r0 = pl.ds(pl.multiple_of(lax.rem(at, jnp.int32(rows)), piece), piece)
                for n in range(top_pieces + 1):
                    src = ref.at[:, pl.ds(n * share + a * piece, piece)]
                    col = pl.ds(pl.multiple_of(base + n * part, part), part)
                    jobs.append((None, src, outs[0].at[t, :, r0, col]))
        return jobs

    (top_half,) = move(
        after([top_got[k] for k in keys], contrib),
        [shaped(nt, nz, rows, groups * group_wide)],
        plan_top,
        nl * groups * (share // piece) * (top_pieces + 1),
        "place_top",
    )
    top_half = after(top_half, contrib)
    top_parts = [top_half] + [grid.from_c(top_half, 0, dh) for dh in range(1, parts)]

    def plan_upper(ins, outs):
        return [(None, ins[0].at[grid.s], outs[0])] + [
            (None, ins[0].at[other(ds)], outs[ds]) for ds in range(1, groups)
        ]

    ups = move(
        [after(upper_panel[0], lower[3])],
        [shaped(count, rows, top_wide)] * groups,
        plan_upper,
        groups,
        "pack_upper",
        args=1,
    )
    up = {(0, 0): ups[0]}

    total = contrib
    if nl * groups <= 4:
        for dl in range(nl):
            for ds in range(groups):
                if dl or ds:
                    pairs = [
                        (
                            ((j + dl) % nl) * nc
                            + ((c // parts + ds) % groups) * parts
                            + c % parts,
                            j * nc + c,
                        )
                        for j in range(nl)
                        for c in range(nc)
                    ]
                    total = total + lax.ppermute(contrib, ("leaf", "pcol"), pairs)
    else:
        for ds in range(1, groups):
            total = total + grid.from_c(contrib, ds, 0)
        total = lax.psum(total, "leaf")
    sent = side - total
    for ds in range(1, groups):
        up[ds, 0] = grid.from_c(after(ups[ds], sent), ds, 0)
    pieces = grid.gather_z(after(sent, top_parts))
    back = after(back, sent)
    back = [back] + [grid.from_c(back, 0, dh) for dh in range(1, parts)]
    for ds in range(groups):
        for dh in range(1, parts):
            up[ds, dh] = grid.from_c(after(up[ds, 0], pieces), 0, dh)

    def top_body(*refs):
        got = refs[:nz]
        halves = refs[nz : nz + parts]
        x_ref, r_scr, y_scr = refs[nz + parts :]
        for d in range(nz):
            for t in range(nt):
                r_scr[t, rows_at(d)] = got[d][t * rows : (t + 1) * rows]

        def solve(h):
            def q_block(t, u):
                c, at = u // top_owned, u % top_owned * nb
                at += c // parts * group_wide
                return halves[(c % parts - h) % parts][t, :, :, at : at + nb].reshape(nb, nb)

            def inv_dot(t, upper, r, out):
                for n in range(nb // part):
                    c = upper * (nb // part) + n
                    at = c // parts * group_wide + top_wide
                    a = halves[(c % parts - h) % parts][t, :, :, at : at + part]
                    out[t, n * part : (n + 1) * part] = dot_t(a.reshape(nb, part), r)

            for t in range(nt):
                r = r_scr[t]
                for u in range(t):
                    r = r - dot(q_block(t, u), y_scr[u])
                inv_dot(t, 0, r, y_scr)
            for t in range(nt - 1, -1, -1):
                r = y_scr[t]
                for u in range(t + 1, nt):
                    r = r - dot(q_block(t, u), x_ref[u])
                inv_dot(t, 1, r, x_ref)

        for h in range(parts):
            pl.when(grid.h == h)(functools.partial(solve, h))

    (top_x,) = call(
        top_body,
        after(pieces, [up[ds, 0] for ds in range(1, groups)]) + top_parts,
        [VMEM] * (nz + parts),
        [shaped(nt, nb, cols)],
        [VMEM],
        [pltpu.VMEM((nt, nz * rows, cols), F32), pltpu.VMEM((nt, nb, cols), F32)],
        "top_sweeps",
        20,
    )

    def couple_body(*refs):
        srcs, x_ref, mask = refs[:nsrc], refs[nsrc], refs[nsrc + 1]
        known = refs[nsrc + 2 : nsrc + 2 + count]
        tiles, sent, scr, m_scr, sem = refs[nsrc + 2 + count :]
        jobs = [
            (None, ref, scr.at[grid.block(ds, dh)]) for (ds, dh), ref in zip(grid.moves, srcs)
        ]
        start_all(jobs, sem)
        for t in range(nt):
            m_scr[pl.ds(t * nb, nb)] = x_ref[t] * mask[t]
        wait_all(jobs, sem)
        acc = None
        for c in range(nc):
            a = scr[c].reshape(count * rows, top_wide)
            term = dot(a, m_scr[pl.ds(c * top_wide, top_wide)])
            acc = term if acc is None else acc + term
        at = pl.ds(pl.multiple_of(grid.z * rows, rows), rows)
        for i in range(count):
            tile = known[i][at] - acc[i * rows : (i + 1) * rows]
            tiles[i] = tile
            if i >= count - owned:
                sent[pl.ds((count - 1 - i) * rows, rows)] = tile

    tiles, sent = call(
        couple_body,
        [up[m] for m in grid.moves] + [top_x, present] + lower,
        [ANY] * nsrc + [VMEM, SMEM] + [VMEM] * count,
        [shaped(count, rows, cols), shaped(owned * rows, cols)],
        [VMEM, VMEM],
        [
            pltpu.VMEM((nc, count, rows, top_wide), F32),
            pltpu.VMEM((nt * nb, cols), F32),
            pltpu.SemaphoreType.DMA((nsrc,)),
        ],
        "coupling",
        4,
    )

    def backward_step(p, pieces, solved):
        g = nc - 1 - p
        last = p == 0
        mine = [p * owned + owned - 1 - n for n in range(owned)]
        nxt = [] if last else [m - owned for m in mine]
        known_ids = sorted(solved)
        ins = list(pieces) + back + [solved[k] for k in known_ids]
        nout = 1 if last else 2
        specs = (
            [VMEM] * nz
            + [ANY] * parts
            + [VMEM] * len(known_ids)
        )
        if not last:
            for i in nxt:
                ins += [a for a, _ in row_sources(i)]
                specs += [ANY] * nsrc
            ins.append(tiles)
            specs.append(VMEM)

        def body(*refs):
            got, inv = refs[:nz], refs[nz : nz + parts]
            known = []
            for k, ref in zip(known_ids, refs[nz + parts : nz + parts + len(known_ids)]):
                known += [(k * owned + n, ref.at[n]) for n in range(owned)]
            rest = refs[nz + parts + len(known_ids) : len(ins)]
            outs = refs[len(ins) : len(ins) + nout]
            x_ref = outs[0]
            r_scr, i_scr, f_scr, sem, i_sem = refs[-5:]
            size = per * part
            inv_jobs = [
                (None, inv[e].at[:, :, pl.ds(g * size, size)], i_scr.at[e]) for e in range(parts)
            ]
            start_all(inv_jobs, i_sem)
            jobs = []
            for n, i in enumerate(nxt):
                jobs += fetch(i, rest[n * nsrc : (n + 1) * nsrc], f_scr, n)
            start_all(jobs, sem)
            for d in range(nz):
                for n in range(owned):
                    r_scr[n, rows_at(d)] = got[d][n * rows : (n + 1) * rows]
            wait_all(inv_jobs, i_sem)
            at = owned * part
            for n in range(owned):
                for m in range(n):
                    for e in range(parts):
                        a = i_scr[e, :, :, at : at + part].reshape(nb, part)
                        half = pl.ds(pl.multiple_of(grid.part(e) * part, part), part)
                        r_scr[n] = r_scr[n] - dot(a, x_ref[owned - 1 - m, half])
                    at += part
                for e in range(parts):
                    a = i_scr[e, :, :, n * part : (n + 1) * part].reshape(nb, part)
                    half = pl.ds(pl.multiple_of(grid.part(e) * part, part), part)
                    x_ref[owned - 1 - n, half] = dot_t(a, r_scr[n])
            wait_all(jobs, sem)
            known += [(p * owned + n, x_ref.at[n]) for n in range(owned)]
            for n, i in enumerate(nxt):
                outs[1][pl.ds(n * rows, rows)] = solved_sum(rest[-1][i], f_scr, n, known)

        res = call(
            body,
            ins,
            specs,
            [shaped(owned, nb, cols), shaped(owned * rows, cols)][:nout],
            [VMEM] * nout,
            [
                pltpu.VMEM((owned, nz * rows, cols), F32),
                pltpu.VMEM((parts, nz, rows, per * part), F32),
                pltpu.VMEM((owned, nc, rows, wide), F32),
                pltpu.SemaphoreType.DMA((owned * nsrc,)),
                pltpu.SemaphoreType.DMA((parts,)),
            ],
            "backward_step",
            5,
        )
        solved[p] = res[0]
        return None if last else res[1]

    def dest(ds, dh):
        return lax.rem(grid.s + (groups - ds), jnp.int32(groups)) * parts + lax.rem(
            grid.h + (parts - dh), jnp.int32(parts)
        )

    def from_block(x, ds, dh, targets):
        return lax.ppermute(
            x,
            "pcol",
            [
                (((c // parts + ds) % groups) * parts + (c % parts + dh) % parts, c)
                for c in targets
            ],
        )

    def plan_pairs(ins, outs):
        return [
            (dest(ds, dh) == p, ref, out)
            for (ds, dh), out in zip(grid.moves[1:], outs)
            for p, ref in zip(range(1, nc), ins)
        ]

    solved, got_pairs = {}, {}
    for p in range(nc - 1, -1, -1):
        sent = backward_step(p, grid.gather_z(sent), solved)
        if p == 1:
            pairs = move(
                [solved[q] for q in range(1, nc)],
                [shaped(owned, nb, cols)] * (nsrc - 1),
                plan_pairs,
                (nsrc - 1) * (nc - 1),
                "pack_pairs",
            )
            for m, x in zip(grid.moves[1:], pairs):
                got_pairs[m] = from_block(x, *m, range(1, nc))
    last_pair = {m: from_block(solved[0], *m, [0]) for m in grid.moves[1:]}

    def top_of(c):
        return lax.dynamic_slice_in_dim(top_x, c * top_owned, top_owned, 0)

    outs = [top_of(grid.c)]
    for e in range(1, parts):
        outs.append(grid.from_c(top_of(dest(0, e)), 0, e))
    outs = jnp.stack(outs)
    top_out = jnp.concatenate([pick(outs, (q - grid.h) % parts) for q in range(parts)], axis=2)
    top_out = lax.dynamic_slice_in_dim(top_out, grid.l * top_rhs.shape[2], top_rhs.shape[2], 2)

    def plan_out(ins, outs):
        jobs = []
        for n, (ds, dh) in enumerate(grid.moves):
            side = pl.ds(pl.multiple_of(grid.part(dh) * cols, cols), cols)
            target = outs[0].at[lax.rem(grid.s + ds, jnp.int32(groups)), :, :, side]
            if n == 0:
                jobs += [(grid.c == p, ins[p], target) for p in range(nc)]
            else:
                jobs.append((grid.c == 0, ins[nc + 2 * n - 2], target))
                jobs.append((grid.c != 0, ins[nc + 2 * n - 1], target))
        return jobs

    ins = [solved[p] for p in range(nc)]
    for m in grid.moves[1:]:
        ins += [last_pair[m], got_pairs[m]]
    (sub_out,) = move(ins, [shaped(groups, owned, nb, nrhs)], plan_out, len(ins), "place_out", True)
    return (sub_out[None], top_out)


def solution(mesh):
    placed = (
        P("leaf", None, None, "prow", "pcol"),
        P("leaf", None, None, "prow", None),
        P("leaf", None, None, "prow", None),
        P("leaf", None, "prow", None, "pcol"),
        P("leaf", None, None, "prow", "pcol"),
        P("leaf", None, None),
        P(None, "prow", "pcol"),
        P(None, "prow", None),
        P(None, "prow", None),
        P("leaf", None, None, "prow", None),
        P(None, "prow", "leaf"),
    )
    return jax.shard_map(
        per_device,
        mesh=mesh,
        in_specs=placed,
        out_specs=(P("leaf", None, "pcol", None, None), P("pcol", None, "leaf")),
        check_vma=False,
    )
```

```python
import functools

import jax
import jax.numpy as jnp
from jax import lax
from jax.experimental import pallas as pl
from jax.experimental.pallas import tpu as pltpu
from jax.sharding import PartitionSpec as P

PRECISION = lax.Precision.HIGHEST
VMEM = pl.BlockSpec(memory_space=pltpu.VMEM)
SMEM = pl.BlockSpec(memory_space=pltpu.SMEM)
ANY = pl.BlockSpec(memory_space=pltpu.HBM)
FREE = pl.BlockSpec(memory_space=pltpu.HBM)
ARG = pl.BlockSpec(memory_space=pltpu.HBM)
F32 = jnp.float32
GRANT = 16 * 1024 * 1024


def dot(a, b):
    return lax.dot_general(
        a, b, (((1,), (0,)), ((), ())), precision=PRECISION, preferred_element_type=F32
    )


def dot_t(a, b):
    return lax.dot_general(
        a, b, (((0,), (0,)), ((), ())), precision=PRECISION, preferred_element_type=F32
    )


def shaped(*shape):
    return jax.ShapeDtypeStruct(shape, F32)


def after(x, dep):
    return x if dep is None else lax.optimization_barrier((x, dep))[0]


def pick(stack, index):
    return lax.dynamic_index_in_dim(stack, index, 0, keepdims=False)


class Grid:
    def __init__(self, groups, columns):
        self.nz = lax.axis_size("prow")
        self.nc = lax.axis_size("pcol")
        self.nl = lax.axis_size("leaf")
        self.groups = groups
        self.parts = self.nc // groups
        self.columns = columns // self.parts
        self.moves = [
            (ds, dh) for ds in range(groups) for dh in range(self.parts)
        ]

    @property
    def z(self):
        return lax.axis_index("prow")

    @property
    def c(self):
        return lax.axis_index("pcol")

    @property
    def l(self):
        return lax.axis_index("leaf")

    @property
    def s(self):
        return lax.div(self.c, jnp.int32(self.parts))

    @property
    def h(self):
        return lax.rem(self.c, jnp.int32(self.parts))

    def block(self, ds, dh):
        return lax.rem(self.s + ds, jnp.int32(self.groups)) * self.parts + self.part(dh)

    def part(self, dh):
        return lax.rem(self.h + dh, jnp.int32(self.parts))

    def row(self, d):
        return lax.rem(self.z + d, jnp.int32(self.nz))

    def from_z(self, x, d):
        return lax.ppermute(x, "prow", [((i + d) % self.nz, i) for i in range(self.nz)])

    def from_l(self, x, d):
        return lax.ppermute(x, "leaf", [((i + d) % self.nl, i) for i in range(self.nl)])

    def from_c(self, x, ds, dh):
        g, k = self.groups, self.parts
        return lax.ppermute(
            x,
            "pcol",
            [(((i // k + ds) % g) * k + (i % k + dh) % k, i) for i in range(self.nc)],
        )

    def gather_z(self, x):
        return [x] + [self.from_z(x, d) for d in range(1, self.nz)]


def call(body, ins, specs, outs, out_specs, scratch, name, us):
    ins = [
        pltpu.with_memory_space_constraint(x, pltpu.HBM) if spec in (ANY, ARG, FREE) else x
        for x, spec in zip(ins, specs)
    ]
    return pl.pallas_call(
        body,
        out_shape=tuple(
            pltpu.VMEM(o.shape, o.dtype) if spec is VMEM else o for o, spec in zip(outs, out_specs)
        ),
        in_specs=list(specs),
        out_specs=tuple(out_specs),
        scratch_shapes=list(scratch),
        compiler_params=pltpu.CompilerParams(vmem_limit_bytes=GRANT),
        cost_estimate=pl.CostEstimate(
            flops=int(us * 1.1e9), bytes_accessed=int(us * 3.6e6), transcendentals=0
        ),
        name=name,
    )(*ins)


def start_all(jobs, sem):
    for n, (cond, src, dst) in enumerate(jobs):
        copy = pltpu.make_async_copy(src, dst, sem.at[n])
        if cond is None:
            copy.start()
        else:
            pl.when(cond)(copy.start)


def wait_all(jobs, sem):
    for n, (cond, src, dst) in enumerate(jobs):
        copy = pltpu.make_async_copy(src, dst, sem.at[n])
        if cond is None:
            copy.wait()
        else:
            pl.when(cond)(copy.wait)


def move(ins, outs, plan, many, name, args=0):
    def body(*refs):
        sem = refs[-1]
        jobs = plan(refs[: len(ins)], refs[len(ins) : -1])
        start_all(jobs, sem)
        wait_all(jobs, sem)

    return call(
        body,
        ins,
        [ARG] * args + [ANY] * (len(ins) - args),
        outs,
        [VMEM] * len(outs),
        [pltpu.SemaphoreType.DMA((many,))],
        name,
        1,
    )


def per_device(
    subtree_factor,
    sub_linv,
    sub_uinv,
    lower_panel,
    upper_panel,
    panel_rows,
    upper_level_factor,
    top_linv,
    top_uinv,
    sub_rhs,
    top_rhs,
):
    _, groups, count, rows, nrhs = sub_rhs.shape
    nb = sub_linv.shape[4]
    nt = top_rhs.shape[0]
    grid = Grid(groups, nrhs)
    nz, nc, nl, parts, cols = grid.nz, grid.nc, grid.nl, grid.parts, grid.columns
    owned = subtree_factor.shape[4] // nb
    top_owned = upper_level_factor.shape[2] // nb
    part = nb // parts
    wide = owned * nb
    early = count // 2
    share = nt * rows // nl
    piece = min(share, rows)
    top_wide = upper_level_factor.shape[2]
    top_pieces = top_wide // part
    cut = (count - early) * rows
    factor, linv, uinv = subtree_factor[0], sub_linv[0], sub_uinv[0]
    rhs = sub_rhs[0]

    def own_part(width):
        return pl.ds(pl.multiple_of(grid.h * width, width), width)

    def rows_at(d):
        return pl.ds(pl.multiple_of(grid.row(d) * rows, rows), rows)

    order = list(range(1, count)) + [0]
    chunks = [order[:owned], order[owned : 2 * owned], order[2 * owned :]]
    where = {i: (n, k) for n, chunk in enumerate(chunks) for k, i in enumerate(chunk)}

    def other(ds):
        return lax.rem(grid.s + (groups - ds), jnp.int32(groups))

    def plan_first(ins, outs):
        rhs_, linv_, factor_ = ins
        m0 = outs[0]
        jobs = [
            (None, rhs_.at[grid.s, 0, :, own_part(cols)], m0.at[:, pl.ds(0, cols)]),
            (None, linv_.at[grid.s, 0], m0.at[:, pl.ds(cols, nb)]),
        ]
        for i in range(1, early):
            at = pl.ds(cols + nb + (i - 1) * part, part)
            jobs.append((None, linv_.at[grid.s, i, :, own_part(part)], m0.at[:, at]))
        for ds in range(1, groups):
            for k, i in enumerate(chunks[0]):
                jobs.append((None, factor_.at[other(ds), i], outs[ds].at[k]))
        return jobs

    first = move(
        [rhs, linv, factor],
        [shaped(rows, cols + nb + (early - 1) * part)]
        + [shaped(owned, rows, wide)] * (groups - 1),
        plan_first,
        1 + early + (groups - 1) * owned,
        "pack_first",
        args=3,
    )
    m0 = grid.gather_z(first[0])
    y_got, sources = {}, {}
    for ds in range(1, groups):
        y_got[ds, 0] = grid.from_c(first[ds], ds, 0)

    def plan_second(ins, outs):
        jobs = [(None, ins[0].at[grid.s], outs[0])]
        for ds in range(1, groups):
            for n in range(1, len(chunks)):
                target = outs[(ds - 1) * (len(chunks) - 1) + n]
                for k, i in enumerate(chunks[n]):
                    jobs.append((None, ins[0].at[other(ds), i], target.at[k]))
        return jobs

    second = move(
        [after(factor, first[0])],
        [shaped(count, rows, wide)]
        + [shaped(len(chunk), rows, wide) for chunk in chunks[1:]] * (groups - 1),
        plan_second,
        1 + count * groups,
        "pack_second",
        args=1,
    )
    own = second[0]

    def plan_bulk(ins, outs):
        linv_, top_, tl_, tu_ = ins
        bulk = outs[0]
        jobs = []
        for k in range(count - early):
            jobs.append(
                (
                    None,
                    linv_.at[grid.s, early + k, :, own_part(part)],
                    bulk.at[pl.ds(k * rows, rows)],
                )
            )
        for a in range(share // piece):
            flat = grid.l * share + a * piece
            t = lax.div(flat, jnp.int32(rows))
            at = pl.ds(pl.multiple_of(lax.rem(flat, jnp.int32(rows)), piece), piece)
            for n in range(top_pieces + 1):
                target = bulk.at[pl.ds(cut + n * share + a * piece, piece)]
                if n < top_pieces:
                    jobs.append((None, top_.at[t, at, pl.ds(n * part, part)], target))
                    continue
                low = pl.ds(pl.multiple_of(grid.s * part, part), part)
                jobs.append((grid.h == 0, tl_.at[t, at, low], target))
                jobs.append((grid.h == 1, tu_.at[t, at, low], target))
        return jobs

    (bulk,) = move(
        [linv, upper_level_factor, top_linv, top_uinv],
        [shaped(cut + (top_pieces + 1) * share, part)],
        plan_bulk,
        count - early + (top_pieces + 2) * (share // piece),
        "pack_bulk",
        args=4,
    )
    gathered = lax.all_gather(after(bulk, m0), "prow")

    def plan_core(ins, outs):
        jobs = [(None, ins[0].at[chunks[0][0]], outs[0].at[0])]
        for ds in range(1, groups):
            jobs.append((None, ins[ds], outs[0].at[pl.ds(1 + (ds - 1) * owned, owned)]))
        return jobs

    (core,) = move(
        [own] + after([y_got[ds, 0] for ds in range(1, groups)], (m0, bulk)),
        [shaped(1 + (groups - 1) * owned, rows, wide)],
        plan_core,
        groups,
        "pack_core",
    )
    cores = {dh: grid.from_c(core, 0, dh) for dh in range(1, parts)}

    def start_chunk(n, dep):
        for ds in range(1, groups):
            sent = second[(ds - 1) * (len(chunks) - 1) + n]
            y_got[ds, n] = grid.from_c(after(sent, dep), ds, 0)
        return [y_got[ds, n] for ds in range(1, groups)]

    def share_chunk(n, dep):
        for ds in range(1, groups):
            for dh in range(1, parts):
                y_got[ds, dh, n] = grid.from_c(after(y_got[ds, n], dep), 0, dh)

    def row_sources(i):
        n, k = where[i]
        out = []
        for ds, dh in grid.moves:
            if dh == 0:
                out.append((y_got[ds, n], k) if ds else (own, i))
            elif n == 0 and ds:
                out.append((cores[dh], 1 + (ds - 1) * owned + k))
            elif ds:
                out.append((y_got[ds, dh, n], k))
            else:
                out.append((cores[dh], 0) if i == chunks[0][0] else (sources[0, dh], i))
        return out

    early_inv = []

    def plan_late(ins, outs):
        jobs = [
            (
                None,
                ins[0].at[a, pl.ds(k * rows, rows)],
                outs[0].at[k, pl.ds(a * rows, rows)],
            )
            for a in range(nz)
            for k in range(count - early)
        ]
        size = (top_pieces + 1) * share
        return jobs + [(None, ins[0].at[:, pl.ds(cut, size)], outs[1])]

    late_inv = []

    def place_late(dep):
        mine, top_mine = move(
            [after(gathered, dep)],
            [
                shaped(count - early, nz * rows, part),
                shaped(nz, (top_pieces + 1) * share, part),
            ],
            plan_late,
            nz * (count - early) + 1,
            "place_late",
        )
        late_inv.extend([mine] + [grid.from_c(mine, 0, dh) for dh in range(1, parts)])
        return top_mine

    def inverse_of(i):
        if i < early:
            return early_inv, i - 1
        return late_inv, i - early

    def fetch(i, refs, scratch, slot):
        return [
            (None, ref.at[index], scratch.at[slot, grid.block(ds, dh)])
            for (ds, dh), ref, (_, index) in zip(grid.moves, refs, row_sources(i))
        ]

    def solved_sum(acc, scratch, slot, known):
        for k, x in known:
            acc = acc - dot(
                scratch[slot, k // owned, :, (k % owned) * nb : (k % owned + 1) * nb], x[...]
            )
        return acc

    nsrc = len(grid.moves)

    def forward_step(i, pieces, solved, extra=()):
        last = i == count - 1
        solved = [] if last else solved
        ins, specs = list(pieces), [VMEM] * nz
        if i:
            stack, index = inverse_of(i)
            ins += stack
            specs += [FREE] * parts
        ninv = len(ins) - nz
        ins += solved
        specs += [VMEM] * len(solved)
        if last:
            ins += list(extra)
            specs += [VMEM, VMEM, SMEM] + [ANY] * nsrc
        else:
            ins += [a for a, _ in row_sources(i + 1)] + [rhs]
            specs += [FREE] * nsrc + [ARG]

        def body(*refs):
            got = refs[:nz]
            inv = refs[nz : nz + ninv]
            known = refs[nz + ninv : nz + ninv + len(solved)]
            rest = refs[nz + ninv + len(solved) : len(ins)]
            x_ref, next_ref, own_ref = refs[len(ins) : len(ins) + 3]
            r_scr, i_scr, f_scr, t_scr, p_scr, sem, i_sem = refs[-7:]
            inv_jobs = [
                (None, inv[e].at[index], i_scr.at[:, pl.ds(e * part, part)]) for e in range(ninv)
            ]
            start_all(inv_jobs, i_sem)
            if last:
                jobs = [
                    (
                        grid.block(ds, dh) == nc - 1,
                        ref.at[:, pl.ds((owned - 1) * nb, nb)],
                        p_scr,
                    )
                    for (ds, dh), ref in zip(grid.moves, rest[3:])
                ]
                start_all(jobs, sem)
            else:
                jobs = fetch(i + 1, rest[:nsrc], f_scr, 0)
                jobs.append((None, rest[nsrc].at[grid.s, i + 1, :, own_part(cols)], t_scr))
                start_all(jobs, sem)
            for d in range(nz):
                r_scr[rows_at(d)] = got[d][:, :cols]
                if i == 0:
                    i_scr[rows_at(d)] = got[d][:, cols : cols + nb]
                    for k in range(early - 1):
                        at = cols + nb + k * part
                        refs[len(ins) + 3][k, rows_at(d)] = got[d][:, at : at + part]
            if i == 0:
                x_ref[...] = dot_t(i_scr[...], r_scr[...])
            wait_all(inv_jobs, i_sem)
            for e in range(ninv):
                at = pl.ds(pl.multiple_of(grid.part(e) * part, part), part)
                x_ref[at] = dot_t(i_scr[:, e * part : (e + 1) * part], r_scr[...])
            own_ref[...] = x_ref[rows_at(0)]
            if last:
                wait_all(jobs, sem)
                total = rest[0][...] + dot(p_scr[...], x_ref[...])
                for t in range(nt):
                    at = slice(t * rows, (t + 1) * rows)
                    next_ref[at] = rest[1][at] - total[at] * rest[2][t]
            else:
                wait_all(jobs, sem)
                known = list(enumerate(known)) + [(i, x_ref)]
                next_ref[...] = solved_sum(t_scr[...], f_scr, 0, known)

        return call(
            body,
            ins,
            specs,
            [shaped(nb, cols), shaped(nt * rows if last else rows, cols), shaped(rows, cols)]
            + [shaped(early - 1, nz * rows, part)] * (i == 0),
            [VMEM] * (3 + (i == 0)),
            [
                pltpu.VMEM((nz * rows, cols), F32),
                pltpu.VMEM((nz * rows, nb), F32),
                pltpu.VMEM((1, nc, rows, wide), F32),
                pltpu.VMEM((rows, cols), F32),
                pltpu.VMEM((nt * rows, nb) if last else (rows, nb), F32),
                pltpu.SemaphoreType.DMA((nsrc + 1,)),
                pltpu.SemaphoreType.DMA((parts,)),
            ],
            "forward_step",
            4,
        )

    present = lax.dynamic_index_in_dim(panel_rows[0].astype(F32), grid.s, 1, keepdims=False)
    per = owned * (owned + 1) // 2
    def plan_back(ins, outs):
        out = outs[0]
        jobs = []
        for p in range(nc):
            base = (nc - 1 - p) * per * part
            for n in range(owned):
                jobs.append(
                    (
                        None,
                        ins[0].at[grid.s, p * owned + owned - 1 - n, :, own_part(part)],
                        out.at[:, pl.ds(base + n * part, part)],
                    )
                )
        at = 1
        for ds, dh in grid.moves:
            p = grid.block(ds, dh)
            col = pl.ds(pl.multiple_of(nb + grid.h * part, part), part)
            to = pl.ds(pl.multiple_of((nc - 1 - p) * per * part + owned * part, part), part)
            if ds == 0:
                jobs.append((None, ins[at].at[p * owned, :, col], out.at[:, to]))
                at += 1
                continue
            for q in range(nc):
                n, k = where[q * owned]
                if dh and not n:
                    k += 1 + (ds - 1) * owned
                jobs.append((p == q, ins[at + n].at[k, :, col], out.at[:, to]))
            at += len(chunks)
        return jobs

    def pack_back():
        ins = [after(uinv, lower[2])]
        for ds, dh in grid.moves:
            if ds == 0:
                ins.append(own if dh == 0 else sources[0, dh])
            else:
                for n in range(len(chunks)):
                    if dh == 0:
                        ins.append(y_got[ds, n])
                    else:
                        ins.append(y_got[ds, dh, n] if n else cores[dh])
        (back,) = move(
            ins, [shaped(rows, nc * per * part)], plan_back, nc * owned + nsrc * nc, "pack_back", args=1
        )
        return back

    def top_side(dep):
        width = top_rhs.shape[2]
        start = grid.l * width - grid.h * cols
        held = jnp.logical_and(grid.s == 0, jnp.logical_and(start >= 0, start < cols))
        mine = jnp.where(held, after(top_rhs, dep), 0.0)
        if width < cols:
            blank = jnp.zeros((nt, rows, cols), F32)
            at = jnp.clip(start, 0, cols - width)
            mine = lax.dynamic_update_slice_in_dim(blank, mine, at, 2)
        return mine.reshape(nt * rows, cols)

    group_wide = top_wide + part

    def place_top():
        keys = sorted(top_got)

        def plan_top(ins, outs):
            jobs = []
            for (dl, ds), ref in zip(keys, ins):
                sg = lax.rem(grid.s + ds, jnp.int32(groups))
                flat = lax.rem(grid.l + dl, jnp.int32(nl)) * share
                for a in range(share // piece):
                    at = flat + a * piece
                    t = lax.div(at, jnp.int32(rows))
                    r0 = pl.ds(pl.multiple_of(lax.rem(at, jnp.int32(rows)), piece), piece)
                    for n in range(top_pieces + 1):
                        src = ref.at[:, pl.ds(n * share + a * piece, piece)]
                        col = sg * top_wide + n * part
                        if n == top_pieces:
                            col = groups * top_wide + sg * part
                        col = pl.ds(pl.multiple_of(col, part), part)
                        jobs.append((None, src, outs[0].at[t, :, r0, col]))
            return jobs

        return move(
            [top_got[k] for k in keys],
            [shaped(nt, nz, rows, groups * group_wide)],
            plan_top,
            nl * groups * (share // piece) * (top_pieces + 1),
            "place_top",
        )[0]

    lower, lower_tiles = [], []
    lp, top_got = {}, {}
    panel = lower_panel[0]

    def panel_of(s, dep):
        x = lax.dynamic_index_in_dim(panel, after(s, dep), 2, keepdims=False)
        return x.reshape(nt * rows, wide)

    pieces = m0
    for i in range(count):
        due = []
        if i == 0:
            for dh in range(1, parts):
                sources[0, dh] = grid.from_c(own, 0, dh)
                due.append(sources[0, dh])
        if i == 1:
            early_inv.extend(
                [mine_early] + [grid.from_c(mine_early, 0, dh) for dh in range(1, parts)]
            )
            due += start_chunk(1, lower[0])
        if i == 2:
            share_chunk(1, lower[1])
            in_flight = start_chunk(2, lower[1])
        if i == early - 1:
            due += in_flight
            share_chunk(2, lower[-1])
            top_mine = place_late((lower[-1], pieces))
            top_got[0, 0] = top_mine
        if i == early:
            held = (lower[-1], late_inv, [v for k, v in y_got.items() if len(k) == 3])
            for dl in range(1, nl):
                top_got[dl, 0] = grid.from_l(after(top_mine, held), dl)
            for ds in range(1, groups):
                top_got[0, ds] = grid.from_c(after(top_mine, held), ds, 0)
        if i == early - 2:
            side = top_side(lower[-1])
        if i == early + 1:
            due += [top_got[k] for k in top_got if any(k)]
            back = pack_back()
            due.append(back)
            back = lax.all_gather(back, "prow")
        if i == early + 2:
            for ds in range(1, groups):
                for dl in range(1, nl):
                    top_got[dl, ds] = grid.from_l(after(top_got[0, ds], lower[-1]), dl)
            lp[0, 0] = panel_of(grid.s, lower[2])
            for ds in range(1, groups):
                lp[ds, 0] = grid.from_c(after(panel_of(other(ds), lower[2]), lower[-1]), ds, 0)
            due += [lp[ds, 0] for ds in range(1, groups)]
        if i == count - 1:
            due.append(back)
        if i == count - 1:
            top_half = place_top()
            due.append(top_half)
        pieces = after(pieces, due)
        if i == count - 1:
            def panel_body(*refs):
                srcs, known = refs[:nsrc], refs[nsrc : nsrc + count - 1]
                total, scr, sem = refs[nsrc + count - 1 :]
                jobs = [
                    (None, ref, scr.at[grid.block(ds, dh)])
                    for (ds, dh), ref in zip(grid.moves, srcs)
                ]
                start_all(jobs, sem)
                wait_all(jobs, sem)
                acc = None
                for k, x in enumerate(known):
                    a = scr[k // owned, :, (k % owned) * nb : (k % owned + 1) * nb]
                    term = dot(a, x[...])
                    acc = term if acc is None else acc + term
                total[...] = acc

            for ds in range(groups):
                for dh in range(1, parts):
                    lp[ds, dh] = grid.from_c(after(lp[ds, 0], lower[-1]), 0, dh)
            (total,) = call(
                panel_body,
                [lp[m] for m in grid.moves] + lower,
                [ANY] * nsrc + [VMEM] * (count - 1),
                [shaped(nt * rows, cols)],
                [VMEM],
                [pltpu.VMEM((nc, nt * rows, wide), F32), pltpu.SemaphoreType.DMA((nsrc,))],
                "panel_sums",
                3,
            )
            x, contrib, tile = forward_step(i, pieces, lower, [total, side, present] + [lp[m] for m in grid.moves])
        else:
            x, sent, tile, *rest = forward_step(i, pieces, lower)
            if i == 0:
                mine_early = rest[0]
            pieces = grid.gather_z(sent)
        lower.append(x)
        lower_tiles.append(tile)


    total, arrived = contrib, []
    if nl * groups <= 4:
        for dl in range(nl):
            for ds in range(groups):
                if dl or ds:
                    pairs = [
                        (
                            ((j + dl) % nl) * nc
                            + ((c // parts + ds) % groups) * parts
                            + c % parts,
                            j * nc + c,
                        )
                        for j in range(nl)
                        for c in range(nc)
                    ]
                    arrived.append(lax.ppermute(contrib, ("leaf", "pcol"), pairs))
        for x in arrived:
            total = total + x
    else:
        for ds in range(1, groups):
            total = total + grid.from_c(contrib, ds, 0)
        total = lax.psum(total, "leaf")
    top_half = after(top_half, contrib)
    top_parts = [top_half] + [grid.from_c(top_half, 0, dh) for dh in range(1, parts)]

    def plan_upper(ins, outs):
        return [(None, ins[0].at[grid.s], outs[0])] + [
            (None, ins[0].at[other(ds)], outs[ds]) for ds in range(1, groups)
        ]

    ups = move(
        [after(upper_panel[0], lower[3])],
        [shaped(count, rows, top_wide)] * groups,
        plan_upper,
        groups,
        "pack_upper",
        args=1,
    )
    up = {(0, 0): ups[0]}

    sent = total
    for ds in range(1, groups):
        up[ds, 0] = grid.from_c(after(ups[ds], sent), ds, 0)
    pieces = grid.gather_z(after(sent, top_parts))
    back = after(back, sent)
    back = [back] + [grid.from_c(back, 0, dh) for dh in range(1, parts)]
    for ds in range(groups):
        for dh in range(1, parts):
            up[ds, dh] = grid.from_c(after(up[ds, 0], pieces), 0, dh)

    def top_body(*refs):
        got = refs[:nz]
        halves = refs[nz : nz + parts]
        x_ref, r_scr, y_scr = refs[nz + parts :]
        for d in range(nz):
            for t in range(nt):
                r_scr[t, rows_at(d)] = got[d][t * rows : (t + 1) * rows]

        def solve(h):
            def q_block(t, u):
                c, at = u // top_owned, u % top_owned * nb
                at += c // parts * top_wide
                return halves[(c % parts - h) % parts][t, :, :, at : at + nb].reshape(nb, nb)

            def inv_dot(t, upper, r, out):
                a = halves[(upper - h) % parts][t, :, :, groups * top_wide :]
                out[t] = dot_t(a.reshape(nb, nb), r)

            for t in range(nt):
                r = r_scr[t]
                for u in range(t):
                    r = r - dot(q_block(t, u), y_scr[u])
                inv_dot(t, 0, r, y_scr)
            for t in range(nt - 1, -1, -1):
                r = y_scr[t]
                for u in range(t + 1, nt):
                    r = r - dot(q_block(t, u), x_ref[u])
                inv_dot(t, 1, r, x_ref)

        for h in range(parts):
            pl.when(grid.h == h)(functools.partial(solve, h))

    (top_x,) = call(
        top_body,
        after(pieces, [up[ds, 0] for ds in range(1, groups)]) + top_parts,
        [VMEM] * (nz + parts),
        [shaped(nt, nb, cols)],
        [VMEM],
        [pltpu.VMEM((nt, nz * rows, cols), F32), pltpu.VMEM((nt, nb, cols), F32)],
        "top_sweeps",
        20,
    )

    def couple_body(*refs):
        srcs, x_ref, mask = refs[:nsrc], refs[nsrc], refs[nsrc + 1]
        known = refs[nsrc + 2 : nsrc + 2 + count]
        tiles, sent, scr, m_scr, sem = refs[nsrc + 2 + count :]
        jobs = [
            (None, ref, scr.at[grid.block(ds, dh)]) for (ds, dh), ref in zip(grid.moves, srcs)
        ]
        start_all(jobs, sem)
        for t in range(nt):
            m_scr[pl.ds(t * nb, nb)] = x_ref[t] * mask[t]
        wait_all(jobs, sem)
        acc = None
        for c in range(nc):
            a = scr[c].reshape(count * rows, top_wide)
            term = dot(a, m_scr[pl.ds(c * top_wide, top_wide)])
            acc = term if acc is None else acc + term
        for i in range(count):
            tile = known[i][...] - acc[i * rows : (i + 1) * rows]
            tiles[i] = tile
            if i >= count - owned:
                sent[pl.ds((count - 1 - i) * rows, rows)] = tile

    tiles, sent = call(
        couple_body,
        [up[m] for m in grid.moves] + [top_x, present] + lower_tiles,
        [ANY] * nsrc + [VMEM, SMEM] + [VMEM] * count,
        [shaped(count, rows, cols), shaped(owned * rows, cols)],
        [VMEM, VMEM],
        [
            pltpu.VMEM((nc, count, rows, top_wide), F32),
            pltpu.VMEM((nt * nb, cols), F32),
            pltpu.SemaphoreType.DMA((nsrc,)),
        ],
        "coupling",
        4,
    )

    def backward_step(p, pieces, solved):
        g = nc - 1 - p
        last = p == 0
        mine = [p * owned + owned - 1 - n for n in range(owned)]
        nxt = [] if last else [m - owned for m in mine]
        known_ids = sorted(solved)
        ins = list(pieces) + back + [solved[k] for k in known_ids]
        nout = 1 if last else 2
        specs = (
            [VMEM] * nz
            + [ANY] * parts
            + [VMEM] * len(known_ids)
        )
        if not last:
            for i in nxt:
                ins += [a for a, _ in row_sources(i)]
                specs += [FREE] * nsrc
            ins.append(tiles)
            specs.append(VMEM)

        def body(*refs):
            got, inv = refs[:nz], refs[nz : nz + parts]
            known = []
            for k, ref in zip(known_ids, refs[nz + parts : nz + parts + len(known_ids)]):
                known += [(k * owned + n, ref.at[n]) for n in range(owned)]
            rest = refs[nz + parts + len(known_ids) : len(ins)]
            outs = refs[len(ins) : len(ins) + nout]
            x_ref = outs[0]
            r_scr, i_scr, f_scr, sem, i_sem = refs[-5:]
            size = per * part
            inv_jobs = [
                (None, inv[e].at[:, :, pl.ds(g * size, size)], i_scr.at[e]) for e in range(parts)
            ]
            start_all(inv_jobs, i_sem)
            jobs = []
            for n, i in enumerate(nxt):
                jobs += fetch(i, rest[n * nsrc : (n + 1) * nsrc], f_scr, n)
            start_all(jobs, sem)
            for d in range(nz):
                for n in range(owned):
                    r_scr[n, rows_at(d)] = got[d][n * rows : (n + 1) * rows]
            wait_all(inv_jobs, i_sem)
            at = owned * part
            for n in range(owned):
                for m in range(n):
                    for e in range(parts):
                        a = i_scr[e, :, :, at : at + part].reshape(nb, part)
                        half = pl.ds(pl.multiple_of(grid.part(e) * part, part), part)
                        r_scr[n] = r_scr[n] - dot(a, x_ref[owned - 1 - m, half])
                    at += part
                for e in range(parts):
                    a = i_scr[e, :, :, n * part : (n + 1) * part].reshape(nb, part)
                    half = pl.ds(pl.multiple_of(grid.part(e) * part, part), part)
                    x_ref[owned - 1 - n, half] = dot_t(a, r_scr[n])
            wait_all(jobs, sem)
            known += [(p * owned + n, x_ref.at[n]) for n in range(owned)]
            for n, i in enumerate(nxt):
                outs[1][pl.ds(n * rows, rows)] = solved_sum(rest[-1][i], f_scr, n, known)

        res = call(
            body,
            ins,
            specs,
            [shaped(owned, nb, cols), shaped(owned * rows, cols)][:nout],
            [VMEM] * nout,
            [
                pltpu.VMEM((owned, nz * rows, cols), F32),
                pltpu.VMEM((parts, nz, rows, per * part), F32),
                pltpu.VMEM((owned, nc, rows, wide), F32),
                pltpu.SemaphoreType.DMA((owned * nsrc,)),
                pltpu.SemaphoreType.DMA((parts,)),
            ],
            "backward_step",
            5,
        )
        solved[p] = res[0]
        return None if last else res[1]

    def dest(ds, dh):
        return lax.rem(grid.s + (groups - ds), jnp.int32(groups)) * parts + lax.rem(
            grid.h + (parts - dh), jnp.int32(parts)
        )

    def from_block(x, ds, dh, targets):
        return lax.ppermute(
            x,
            "pcol",
            [
                (((c // parts + ds) % groups) * parts + (c % parts + dh) % parts, c)
                for c in targets
            ],
        )

    def plan_pairs(ins, outs):
        return [
            (dest(ds, dh) == p, ref, out)
            for (ds, dh), out in zip(grid.moves[1:], outs)
            for p, ref in zip(range(1, nc), ins)
        ]

    solved, got_pairs = {}, {}
    for p in range(nc - 1, -1, -1):
        sent = backward_step(p, grid.gather_z(sent), solved)
        if p == 1:
            pairs = move(
                [solved[q] for q in range(1, nc)],
                [shaped(owned, nb, cols)] * (nsrc - 1),
                plan_pairs,
                (nsrc - 1) * (nc - 1),
                "pack_pairs",
            )
            for m, x in zip(grid.moves[1:], pairs):
                got_pairs[m] = from_block(x, *m, range(1, nc))
    last_pair = {m: from_block(solved[0], *m, [0]) for m in grid.moves[1:]}

    def top_of(c):
        return lax.dynamic_slice_in_dim(top_x, c * top_owned, top_owned, 0)

    outs = [top_of(grid.c)]
    for e in range(1, parts):
        outs.append(grid.from_c(top_of(dest(0, e)), 0, e))
    outs = jnp.stack(outs)
    top_out = jnp.concatenate([pick(outs, (q - grid.h) % parts) for q in range(parts)], axis=2)
    top_out = lax.dynamic_slice_in_dim(top_out, grid.l * top_rhs.shape[2], top_rhs.shape[2], 2)

    def plan_out(ins, outs):
        jobs = []
        for n, (ds, dh) in enumerate(grid.moves):
            side = pl.ds(pl.multiple_of(grid.part(dh) * cols, cols), cols)
            target = outs[0].at[lax.rem(grid.s + ds, jnp.int32(groups)), :, :, side]
            if n == 0:
                jobs += [(grid.c == p, ins[p], target) for p in range(nc)]
            else:
                jobs.append((grid.c == 0, ins[nc + 2 * n - 2], target))
                jobs.append((grid.c != 0, ins[nc + 2 * n - 1], target))
        return jobs

    ins = [solved[p] for p in range(nc)]
    for m in grid.moves[1:]:
        ins += [last_pair[m], got_pairs[m]]
    def out_body(*refs):
        sem = refs[-1]
        jobs = plan_out(refs[: len(ins)], refs[len(ins) : -1])
        start_all(jobs, sem)
        wait_all(jobs, sem)

    (sub_out,) = call(
        out_body,
        ins,
        [VMEM] * len(ins),
        [shaped(groups, owned, nb, nrhs)],
        [ANY],
        [pltpu.SemaphoreType.DMA((len(ins),))],
        "place_out",
        1,
    )
    return (sub_out[None], top_out)


def solution(mesh):
    placed = (
        P("leaf", None, None, "prow", "pcol"),
        P("leaf", None, None, "prow", None),
        P("leaf", None, None, "prow", None),
        P("leaf", None, "prow", None, "pcol"),
        P("leaf", None, None, "prow", "pcol"),
        P("leaf", None, None),
        P(None, "prow", "pcol"),
        P(None, "prow", None),
        P(None, "prow", None),
        P("leaf", None, None, "prow", None),
        P(None, "prow", "leaf"),
    )
    return jax.shard_map(
        per_device,
        mesh=mesh,
        in_specs=placed,
        out_specs=(P("leaf", None, "pcol", None, None), P("pcol", None, "leaf")),
        check_vma=False,
    )
```

```python
import functools

import jax
import jax.numpy as jnp
from jax import lax
from jax.experimental import pallas as pl
from jax.experimental.pallas import tpu as pltpu
from jax.sharding import PartitionSpec as P

PRECISION = lax.Precision.HIGHEST
VMEM = pl.BlockSpec(memory_space=pltpu.VMEM)
SMEM = pl.BlockSpec(memory_space=pltpu.SMEM)
ANY = pl.BlockSpec(memory_space=pltpu.HBM)
FREE = pl.BlockSpec(memory_space=pltpu.HBM)
ARG = pl.BlockSpec(memory_space=pltpu.HBM)
F32 = jnp.float32
GRANT = 16 * 1024 * 1024


def dot(a, b):
    return lax.dot_general(
        a, b, (((1,), (0,)), ((), ())), precision=PRECISION, preferred_element_type=F32
    )


def dot_t(a, b):
    return lax.dot_general(
        a, b, (((0,), (0,)), ((), ())), precision=PRECISION, preferred_element_type=F32
    )


def shaped(*shape):
    return jax.ShapeDtypeStruct(shape, F32)


def after(x, dep):
    return x if dep is None else lax.optimization_barrier((x, dep))[0]


def pick(stack, index):
    return lax.dynamic_index_in_dim(stack, index, 0, keepdims=False)


class Grid:
    def __init__(self, groups, columns):
        self.nz = lax.axis_size("prow")
        self.nc = lax.axis_size("pcol")
        self.nl = lax.axis_size("leaf")
        self.groups = groups
        self.parts = self.nc // groups
        self.columns = columns // self.parts
        self.moves = [
            (ds, dh) for ds in range(groups) for dh in range(self.parts)
        ]

    @property
    def z(self):
        return lax.axis_index("prow")

    @property
    def c(self):
        return lax.axis_index("pcol")

    @property
    def l(self):
        return lax.axis_index("leaf")

    @property
    def s(self):
        return lax.div(self.c, jnp.int32(self.parts))

    @property
    def h(self):
        return lax.rem(self.c, jnp.int32(self.parts))

    def block(self, ds, dh):
        return lax.rem(self.s + ds, jnp.int32(self.groups)) * self.parts + self.part(dh)

    def part(self, dh):
        return lax.rem(self.h + dh, jnp.int32(self.parts))

    def row(self, d):
        return lax.rem(self.z + d, jnp.int32(self.nz))

    def from_z(self, x, d):
        return lax.ppermute(x, "prow", [((i + d) % self.nz, i) for i in range(self.nz)])

    def from_l(self, x, d):
        return lax.ppermute(x, "leaf", [((i + d) % self.nl, i) for i in range(self.nl)])

    def from_c(self, x, ds, dh):
        g, k = self.groups, self.parts
        return lax.ppermute(
            x,
            "pcol",
            [(((i // k + ds) % g) * k + (i % k + dh) % k, i) for i in range(self.nc)],
        )

    def gather_z(self, x):
        return [x] + [self.from_z(x, d) for d in range(1, self.nz)]


def call(body, ins, specs, outs, out_specs, scratch, name, us):
    ins = [
        pltpu.with_memory_space_constraint(x, pltpu.HBM) if spec in (ANY, ARG, FREE) else x
        for x, spec in zip(ins, specs)
    ]
    return pl.pallas_call(
        body,
        out_shape=tuple(
            pltpu.VMEM(o.shape, o.dtype) if spec is VMEM else o for o, spec in zip(outs, out_specs)
        ),
        in_specs=list(specs),
        out_specs=tuple(out_specs),
        scratch_shapes=list(scratch),
        compiler_params=pltpu.CompilerParams(vmem_limit_bytes=GRANT),
        cost_estimate=pl.CostEstimate(
            flops=int(us * 1.1e9), bytes_accessed=int(us * 3.6e6), transcendentals=0
        ),
        name=name,
    )(*ins)


def start_all(jobs, sem):
    for n, (cond, src, dst) in enumerate(jobs):
        copy = pltpu.make_async_copy(src, dst, sem.at[n])
        if cond is None:
            copy.start()
        else:
            pl.when(cond)(copy.start)


def wait_all(jobs, sem):
    for n, (cond, src, dst) in enumerate(jobs):
        copy = pltpu.make_async_copy(src, dst, sem.at[n])
        if cond is None:
            copy.wait()
        else:
            pl.when(cond)(copy.wait)


def move(ins, outs, plan, many, name, args=0, near=False):
    def body(*refs):
        sem = refs[-1]
        jobs = plan(refs[: len(ins)], refs[len(ins) : -1])
        start_all(jobs, sem)
        wait_all(jobs, sem)

    return call(
        body,
        ins,
        [ARG] * args + [VMEM if near else ANY] * (len(ins) - args),
        outs,
        [VMEM] * len(outs),
        [pltpu.SemaphoreType.DMA((many,))],
        name,
        1,
    )


def per_device(
    subtree_factor,
    sub_linv,
    sub_uinv,
    lower_panel,
    upper_panel,
    panel_rows,
    upper_level_factor,
    top_linv,
    top_uinv,
    sub_rhs,
    top_rhs,
):
    _, groups, count, rows, nrhs = sub_rhs.shape
    nb = sub_linv.shape[4]
    nt = top_rhs.shape[0]
    grid = Grid(groups, nrhs)
    nz, nc, nl, parts, cols = grid.nz, grid.nc, grid.nl, grid.parts, grid.columns
    owned = subtree_factor.shape[4] // nb
    top_owned = upper_level_factor.shape[2] // nb
    part = nb // parts
    wide = owned * nb
    early = count // 2
    share = nt * rows // nl
    piece = min(share, rows)
    top_wide = upper_level_factor.shape[2]
    top_pieces = top_wide // part
    cut = (count - early) * rows
    factor, linv, uinv = subtree_factor[0], sub_linv[0], sub_uinv[0]
    rhs = sub_rhs[0]

    def own_part(width):
        return pl.ds(pl.multiple_of(grid.h * width, width), width)

    def rows_at(d):
        return pl.ds(pl.multiple_of(grid.row(d) * rows, rows), rows)

    order = list(range(1, count)) + [0]
    chunks = [order[:owned], order[owned : 2 * owned], order[2 * owned :]]
    where = {i: (n, k) for n, chunk in enumerate(chunks) for k, i in enumerate(chunk)}

    def other(ds):
        return lax.rem(grid.s + (groups - ds), jnp.int32(groups))

    def plan_first(ins, outs):
        rhs_, linv_, factor_ = ins
        m0 = outs[0]
        jobs = [
            (None, rhs_.at[grid.s, 0, :, own_part(cols)], m0.at[:, pl.ds(0, cols)]),
            (None, linv_.at[grid.s, 0], m0.at[:, pl.ds(cols, nb)]),
        ]
        for i in range(1, early):
            at = pl.ds(cols + nb + (i - 1) * part, part)
            jobs.append((None, linv_.at[grid.s, i, :, own_part(part)], m0.at[:, at]))
        for ds in range(1, groups):
            for k, i in enumerate(chunks[0]):
                jobs.append((None, factor_.at[other(ds), i], outs[ds].at[k]))
        return jobs

    first = move(
        [rhs, linv, factor],
        [shaped(rows, cols + nb + (early - 1) * part)]
        + [shaped(owned, rows, wide)] * (groups - 1),
        plan_first,
        1 + early + (groups - 1) * owned,
        "pack_first",
        args=3,
    )
    m0 = grid.gather_z(first[0])
    y_got, sources = {}, {}
    for ds in range(1, groups):
        y_got[ds, 0] = grid.from_c(first[ds], ds, 0)

    def plan_second(ins, outs):
        jobs = [(None, ins[0].at[grid.s], outs[0])]
        for ds in range(1, groups):
            for n in range(1, len(chunks)):
                target = outs[(ds - 1) * (len(chunks) - 1) + n]
                for k, i in enumerate(chunks[n]):
                    jobs.append((None, ins[0].at[other(ds), i], target.at[k]))
        return jobs

    second = move(
        [after(factor, first[0])],
        [shaped(count, rows, wide)]
        + [shaped(len(chunk), rows, wide) for chunk in chunks[1:]] * (groups - 1),
        plan_second,
        1 + count * groups,
        "pack_second",
        args=1,
    )
    own = second[0]

    def plan_bulk(ins, outs):
        linv_, top_, tl_, tu_ = ins
        bulk = outs[0]
        jobs = []
        for k in range(count - early):
            jobs.append(
                (
                    None,
                    linv_.at[grid.s, early + k, :, own_part(part)],
                    bulk.at[pl.ds(k * rows, rows)],
                )
            )
        for a in range(share // piece):
            flat = grid.l * share + a * piece
            t = lax.div(flat, jnp.int32(rows))
            at = pl.ds(pl.multiple_of(lax.rem(flat, jnp.int32(rows)), piece), piece)
            for n in range(top_pieces + 1):
                target = bulk.at[pl.ds(cut + n * share + a * piece, piece)]
                if n < top_pieces:
                    jobs.append((None, top_.at[t, at, pl.ds(n * part, part)], target))
                    continue
                low = pl.ds(pl.multiple_of(grid.s * part, part), part)
                jobs.append((grid.h == 0, tl_.at[t, at, low], target))
                jobs.append((grid.h == 1, tu_.at[t, at, low], target))
        return jobs

    (bulk,) = move(
        [linv, upper_level_factor, top_linv, top_uinv],
        [shaped(cut + (top_pieces + 1) * share, part)],
        plan_bulk,
        count - early + (top_pieces + 2) * (share // piece),
        "pack_bulk",
        args=4,
    )
    gathered = lax.all_gather(after(bulk, m0), "prow")

    def plan_core(ins, outs):
        jobs = [(None, ins[0].at[chunks[0][0]], outs[0].at[0])]
        for ds in range(1, groups):
            jobs.append((None, ins[ds], outs[0].at[pl.ds(1 + (ds - 1) * owned, owned)]))
        return jobs

    (core,) = move(
        [own] + after([y_got[ds, 0] for ds in range(1, groups)], (m0, bulk)),
        [shaped(1 + (groups - 1) * owned, rows, wide)],
        plan_core,
        groups,
        "pack_core",
        near=True,
    )
    cores = {dh: grid.from_c(core, 0, dh) for dh in range(1, parts)}

    def start_chunk(n, dep):
        for ds in range(1, groups):
            sent = second[(ds - 1) * (len(chunks) - 1) + n]
            y_got[ds, n] = grid.from_c(after(sent, dep), ds, 0)
        return [y_got[ds, n] for ds in range(1, groups)]

    def share_chunk(n, dep):
        for ds in range(1, groups):
            for dh in range(1, parts):
                y_got[ds, dh, n] = grid.from_c(after(y_got[ds, n], dep), 0, dh)

    def row_sources(i):
        n, k = where[i]
        out = []
        for ds, dh in grid.moves:
            if dh == 0:
                out.append((y_got[ds, n], k) if ds else (own, i))
            elif n == 0 and ds:
                out.append((cores[dh], 1 + (ds - 1) * owned + k))
            elif ds:
                out.append((y_got[ds, dh, n], k))
            else:
                out.append((cores[dh], 0) if i == chunks[0][0] else (sources[0, dh], i))
        return out

    early_inv = []

    def plan_late(ins, outs):
        jobs = [
            (
                None,
                ins[0].at[a, pl.ds(k * rows, rows)],
                outs[0].at[k, pl.ds(a * rows, rows)],
            )
            for a in range(nz)
            for k in range(count - early)
        ]
        size = (top_pieces + 1) * share
        return jobs + [(None, ins[0].at[:, pl.ds(cut, size)], outs[1])]

    late_inv = []

    def place_late(dep):
        mine, top_mine = move(
            [after(gathered, dep)],
            [
                shaped(count - early, nz * rows, part),
                shaped(nz, (top_pieces + 1) * share, part),
            ],
            plan_late,
            nz * (count - early) + 1,
            "place_late",
        )
        late_inv.extend([mine] + [grid.from_c(mine, 0, dh) for dh in range(1, parts)])
        return top_mine

    def inverse_of(i):
        if i < early:
            return early_inv, i - 1
        return late_inv, i - early

    def fetch(i, refs, scratch, slot):
        return [
            (None, ref.at[index], scratch.at[slot, grid.block(ds, dh)])
            for (ds, dh), ref, (_, index) in zip(grid.moves, refs, row_sources(i))
        ]

    def solved_sum(acc, scratch, slot, known):
        for k, x in known:
            acc = acc - dot(
                scratch[slot, k // owned, :, (k % owned) * nb : (k % owned + 1) * nb], x[...]
            )
        return acc

    nsrc = len(grid.moves)

    def forward_step(i, pieces, solved, extra=()):
        last = i == count - 1
        solved = [] if last else solved
        ins, specs = list(pieces), [VMEM] * nz
        if i:
            stack, index = inverse_of(i)
            ins += stack
            specs += [FREE] * parts
        ninv = len(ins) - nz
        ins += solved
        specs += [VMEM] * len(solved)
        if last:
            ins += list(extra)
            specs += [VMEM, VMEM, SMEM] + [ANY] * nsrc
        else:
            ins += [a for a, _ in row_sources(i + 1)] + [rhs]
            specs += [FREE] * nsrc + [ARG]

        def body(*refs):
            got = refs[:nz]
            inv = refs[nz : nz + ninv]
            known = refs[nz + ninv : nz + ninv + len(solved)]
            rest = refs[nz + ninv + len(solved) : len(ins)]
            x_ref, next_ref = refs[len(ins) : len(ins) + 2]
            r_scr, i_scr, f_scr, t_scr, p_scr, sem, i_sem = refs[-7:]
            inv_jobs = [
                (None, inv[e].at[index], i_scr.at[:, pl.ds(e * part, part)]) for e in range(ninv)
            ]
            start_all(inv_jobs, i_sem)
            if last:
                jobs = [
                    (
                        grid.block(ds, dh) == nc - 1,
                        ref.at[:, pl.ds((owned - 1) * nb, nb)],
                        p_scr,
                    )
                    for (ds, dh), ref in zip(grid.moves, rest[3:])
                ]
                start_all(jobs, sem)
            else:
                jobs = fetch(i + 1, rest[:nsrc], f_scr, 0)
                jobs.append((None, rest[nsrc].at[grid.s, i + 1, :, own_part(cols)], t_scr))
                start_all(jobs, sem)
            for d in range(nz):
                r_scr[rows_at(d)] = got[d][:, :cols]
                if i == 0:
                    i_scr[rows_at(d)] = got[d][:, cols : cols + nb]
                    for k in range(early - 1):
                        at = cols + nb + k * part
                        refs[len(ins) + 2][k, rows_at(d)] = got[d][:, at : at + part]
            if i == 0:
                x_ref[...] = dot_t(i_scr[...], r_scr[...])
            wait_all(inv_jobs, i_sem)
            for e in range(ninv):
                at = pl.ds(pl.multiple_of(grid.part(e) * part, part), part)
                x_ref[at] = dot_t(i_scr[:, e * part : (e + 1) * part], r_scr[...])
            if last:
                wait_all(jobs, sem)
                total = rest[0][...] + dot(p_scr[...], x_ref[...])
                for t in range(nt):
                    at = slice(t * rows, (t + 1) * rows)
                    next_ref[at] = rest[1][at] - total[at] * rest[2][t]
            else:
                wait_all(jobs, sem)
                known = list(enumerate(known)) + [(i, x_ref)]
                next_ref[...] = solved_sum(t_scr[...], f_scr, 0, known)

        return call(
            body,
            ins,
            specs,
            [shaped(nb, cols), shaped(nt * rows if last else rows, cols)]
            + [shaped(early - 1, nz * rows, part)] * (i == 0),
            [VMEM] * (2 + (i == 0)),
            [
                pltpu.VMEM((nz * rows, cols), F32),
                pltpu.VMEM((nz * rows, nb), F32),
                pltpu.VMEM((1, nc, rows, wide), F32),
                pltpu.VMEM((rows, cols), F32),
                pltpu.VMEM((nt * rows, nb) if last else (rows, nb), F32),
                pltpu.SemaphoreType.DMA((nsrc + 1,)),
                pltpu.SemaphoreType.DMA((parts,)),
            ],
            "forward_step",
            4,
        )

    def forward_stage(i, solved):
        last = i == count - 1
        stack, index = inverse_of(i)
        ins, specs = list(stack), [FREE] * parts
        if last:
            ins += [lp[m] for m in grid.moves]
            specs += [ANY] * nsrc
        else:
            ins += solved + [a for a, _ in row_sources(i + 1)] + [rhs]
            specs += [VMEM] * len(solved) + [FREE] * nsrc + [ARG]

        def body(*refs):
            rest = refs[parts : len(ins)]
            inv_ref, new_ref = refs[len(ins) : len(ins) + 2]
            f_scr, t_scr, sem = refs[-3:]
            jobs = [
                (None, refs[e].at[index], inv_ref.at[:, pl.ds(e * part, part)])
                for e in range(parts)
            ]
            if last:
                at = pl.ds((owned - 1) * nb, nb)
                jobs += [
                    (grid.block(*m) == nc - 1, ref.at[:, at], new_ref)
                    for m, ref in zip(grid.moves, rest)
                ]
            else:
                jobs += fetch(i + 1, rest[len(solved) : -1], f_scr, 0)
                jobs.append((None, rest[-1].at[grid.s, i + 1, :, own_part(cols)], t_scr))
            start_all(jobs, sem)
            wait_all(jobs, sem)
            if not last:
                known = list(enumerate(rest[: len(solved)]))
                refs[len(ins) + 2][...] = solved_sum(t_scr[...], f_scr, 0, known)
                new_ref[...] = f_scr[0, i // owned, :, (i % owned) * nb : (i % owned + 1) * nb]

        outs = [shaped(nz * rows, nb)]
        if last:
            outs.append(shaped(nt * rows, nb))
        else:
            outs += [shaped(rows, nb), shaped(rows, cols)]
        return call(
            body,
            ins,
            specs,
            outs,
            [VMEM] * len(outs),
            [
                pltpu.VMEM((1, nc, rows, wide), F32),
                pltpu.VMEM((rows, cols), F32),
                pltpu.SemaphoreType.DMA((nsrc + 1 + parts,)),
            ],
            "forward_stage",
            1,
        )

    def forward_solve(i, pieces, stage, extra=()):
        last = i == count - 1
        ins = list(pieces) + list(stage) + list(extra)
        specs = [VMEM] * (nz + len(stage)) + [VMEM, VMEM, SMEM] * last

        def body(*refs):
            got, inv_ref, new_ref = refs[:nz], refs[nz], refs[nz + 1]
            rest = refs[nz + 2 : len(ins)]
            x_ref, next_ref, r_scr = refs[len(ins) :]
            for d in range(nz):
                r_scr[rows_at(d)] = got[d][...]
            for e in range(parts):
                at = pl.ds(pl.multiple_of(grid.part(e) * part, part), part)
                x_ref[at] = dot_t(inv_ref[:, e * part : (e + 1) * part], r_scr[...])
            if last:
                total = rest[0][...] + dot(new_ref[...], x_ref[...])
                for t in range(nt):
                    at = slice(t * rows, (t + 1) * rows)
                    next_ref[at] = rest[1][at] - total[at] * rest[2][t]
            else:
                next_ref[...] = rest[0][...] - dot(new_ref[...], x_ref[...])

        return call(
            body,
            ins,
            specs,
            [shaped(nb, cols), shaped(nt * rows if last else rows, cols)],
            [VMEM] * 2,
            [pltpu.VMEM((nz * rows, cols), F32)],
            "forward_solve",
            4,
        )

    present = lax.dynamic_index_in_dim(panel_rows[0].astype(F32), grid.s, 1, keepdims=False)
    per = owned * (owned + 1) // 2
    def plan_back(ins, outs):
        out = outs[0]
        jobs = []
        for p in range(nc):
            base = (nc - 1 - p) * per * part
            for n in range(owned):
                jobs.append(
                    (
                        None,
                        ins[0].at[grid.s, p * owned + owned - 1 - n, :, own_part(part)],
                        out.at[:, pl.ds(base + n * part, part)],
                    )
                )
        at = 1
        for ds, dh in grid.moves:
            p = grid.block(ds, dh)
            col = pl.ds(pl.multiple_of(nb + grid.h * part, part), part)
            to = pl.ds(pl.multiple_of((nc - 1 - p) * per * part + owned * part, part), part)
            if ds == 0:
                jobs.append((None, ins[at].at[p * owned, :, col], out.at[:, to]))
                at += 1
                continue
            for q in range(nc):
                n, k = where[q * owned]
                if dh and not n:
                    k += 1 + (ds - 1) * owned
                jobs.append((p == q, ins[at + n].at[k, :, col], out.at[:, to]))
            at += len(chunks)
        return jobs

    def pack_back():
        ins = [after(uinv, lower[2])]
        for ds, dh in grid.moves:
            if ds == 0:
                ins.append(own if dh == 0 else sources[0, dh])
            else:
                for n in range(len(chunks)):
                    if dh == 0:
                        ins.append(y_got[ds, n])
                    else:
                        ins.append(y_got[ds, dh, n] if n else cores[dh])
        (back,) = move(
            ins, [shaped(rows, nc * per * part)], plan_back, nc * owned + nsrc * nc, "pack_back", args=1
        )
        return back

    def top_side(dep):
        width = top_rhs.shape[2]
        start = grid.l * width - grid.h * cols
        held = jnp.logical_and(grid.s == 0, jnp.logical_and(start >= 0, start < cols))
        mine = jnp.where(held, after(top_rhs, dep), 0.0)
        if width < cols:
            blank = jnp.zeros((nt, rows, cols), F32)
            at = jnp.clip(start, 0, cols - width)
            mine = lax.dynamic_update_slice_in_dim(blank, mine, at, 2)
        return mine.reshape(nt * rows, cols)

    group_wide = top_wide + part

    def place_top(dep):
        keys = sorted(top_got)

        def plan_top(ins, outs):
            jobs = []
            for (dl, ds), ref in zip(keys, ins):
                sg = lax.rem(grid.s + ds, jnp.int32(groups))
                flat = lax.rem(grid.l + dl, jnp.int32(nl)) * share
                for a in range(share // piece):
                    at = flat + a * piece
                    t = lax.div(at, jnp.int32(rows))
                    r0 = pl.ds(pl.multiple_of(lax.rem(at, jnp.int32(rows)), piece), piece)
                    for n in range(top_pieces + 1):
                        src = ref.at[:, pl.ds(n * share + a * piece, piece)]
                        col = sg * top_wide + n * part
                        if n == top_pieces:
                            col = groups * top_wide + sg * part
                        col = pl.ds(pl.multiple_of(col, part), part)
                        jobs.append((None, src, outs[0].at[t, :, r0, col]))
            return jobs

        return move(
            after([top_got[k] for k in keys], dep),
            [shaped(nt, nz, rows, groups * group_wide)],
            plan_top,
            nl * groups * (share // piece) * (top_pieces + 1),
            "place_top",
            near=True,
        )[0]

    def pack_upper(dep):
        def plan_upper(ins, outs):
            return [(None, ins[0].at[grid.s], outs[0])] + [
                (None, ins[0].at[other(ds)], outs[ds]) for ds in range(1, groups)
            ]

        return move(
            [after(upper_panel[0], dep)],
            [shaped(count, rows, top_wide)] * groups,
            plan_upper,
            groups,
            "pack_upper",
            args=1,
        )

    lower = []
    lp, top_got = {}, {}
    panel = lower_panel[0]

    def panel_of(s, dep):
        x = lax.dynamic_index_in_dim(panel, after(s, dep), 2, keepdims=False)
        return x.reshape(nt * rows, wide)

    pieces = m0
    for i in range(count):
        due = []
        if i == 0:
            for dh in range(1, parts):
                sources[0, dh] = grid.from_c(own, 0, dh)
                due.append(sources[0, dh])
        if i == 1:
            early_inv.extend(
                [mine_early] + [grid.from_c(mine_early, 0, dh) for dh in range(1, parts)]
            )
            due += start_chunk(1, lower[0])
        if i == 2:
            share_chunk(1, lower[1])
            in_flight = start_chunk(2, lower[1])
        if i == early - 1:
            due += in_flight
            share_chunk(2, lower[-1])
            top_mine = place_late((lower[-1], pieces))
            top_got[0, 0] = top_mine
        if i == early:
            held = (lower[-1], late_inv, [v for k, v in y_got.items() if len(k) == 3])
            for dl in range(1, nl):
                top_got[dl, 0] = grid.from_l(after(top_mine, held), dl)
            for ds in range(1, groups):
                top_got[0, ds] = grid.from_c(after(top_mine, held), ds, 0)
        if i == early - 2:
            side = top_side(lower[-1])
        if i == early + 1:
            due += [top_got[k] for k in top_got if any(k)]
            back = pack_back()
            due.append(back)
            back = lax.all_gather(back, "prow")
        if i == early + 2:
            for ds in range(1, groups):
                for dl in range(1, nl):
                    top_got[dl, ds] = grid.from_l(after(top_got[0, ds], lower[-1]), dl)
            lp[0, 0] = panel_of(grid.s, lower[2])
            for ds in range(1, groups):
                lp[ds, 0] = grid.from_c(after(panel_of(other(ds), lower[2]), lower[-1]), ds, 0)
            due += [lp[ds, 0] for ds in range(1, groups)]
        if i == count - 1:
            due.append(back)
            ups = pack_upper(lower[-1])
            due += list(ups)
        pieces = after(pieces, due)
        if i == count - 1:
            def panel_body(*refs):
                srcs, known = refs[:nsrc], refs[nsrc : nsrc + count - 1]
                total, scr, sem = refs[nsrc + count - 1 :]
                jobs = [
                    (None, ref, scr.at[grid.block(ds, dh)])
                    for (ds, dh), ref in zip(grid.moves, srcs)
                ]
                start_all(jobs, sem)
                wait_all(jobs, sem)
                acc = None
                for k, x in enumerate(known):
                    a = scr[k // owned, :, (k % owned) * nb : (k % owned + 1) * nb]
                    term = dot(a, x[...])
                    acc = term if acc is None else acc + term
                total[...] = acc

            for ds in range(groups):
                for dh in range(1, parts):
                    lp[ds, dh] = grid.from_c(after(lp[ds, 0], lower[-1]), 0, dh)
            (total,) = call(
                panel_body,
                [lp[m] for m in grid.moves] + lower,
                [ANY] * nsrc + [VMEM] * (count - 1),
                [shaped(nt * rows, cols)],
                [VMEM],
                [pltpu.VMEM((nc, nt * rows, wide), F32), pltpu.SemaphoreType.DMA((nsrc,))],
                "panel_sums",
                3,
            )
            stage = forward_stage(i, lower)
            x, contrib = forward_solve(i, pieces, stage, [total, side, present])
        else:
            if i:
                x, sent = forward_solve(i, pieces, forward_stage(i, lower))
            else:
                x, sent, *rest = forward_step(i, pieces, lower)
            if i == 0:
                mine_early = rest[0]
            pieces = grid.gather_z(sent)
        lower.append(x)


    def tiles_body(*refs):
        for i in range(count):
            refs[count][i] = refs[i][rows_at(0)]

    (lower_tiles,) = call(
        tiles_body,
        lower[:-1] + [after(lower[-1], contrib)],
        [VMEM] * count,
        [shaped(count, rows, cols)],
        [VMEM],
        [],
        "row_tiles",
        1,
    )
    total, arrived = contrib, []
    if nl * groups <= 4:
        for dl in range(nl):
            for ds in range(groups):
                if dl or ds:
                    pairs = [
                        (
                            ((j + dl) % nl) * nc
                            + ((c // parts + ds) % groups) * parts
                            + c % parts,
                            j * nc + c,
                        )
                        for j in range(nl)
                        for c in range(nc)
                    ]
                    arrived.append(lax.ppermute(contrib, ("leaf", "pcol"), pairs))
        for x in arrived:
            total = total + x
    else:
        for ds in range(1, groups):
            total = total + grid.from_c(contrib, ds, 0)
        total = lax.psum(total, "leaf")
    up = {(0, 0): ups[0]}

    sent = after(total, lower_tiles)
    for ds in range(1, groups):
        up[ds, 0] = grid.from_c(after(ups[ds], sent), ds, 0)
    top_half = place_top(sent)
    top_parts = [top_half] + [grid.from_c(top_half, 0, dh) for dh in range(1, parts)]
    pieces = grid.gather_z(after(sent, top_half))
    back = after(back, sent)
    back = [back] + [grid.from_c(back, 0, dh) for dh in range(1, parts)]
    for ds in range(groups):
        for dh in range(1, parts):
            up[ds, dh] = grid.from_c(after(up[ds, 0], pieces), 0, dh)

    def top_body(*refs):
        got = refs[:nz]
        halves = refs[nz : nz + parts]
        x_ref, r_scr, y_scr = refs[nz + parts :]
        for d in range(nz):
            for t in range(nt):
                r_scr[t, rows_at(d)] = got[d][t * rows : (t + 1) * rows]

        def solve(h):
            def q_block(t, u):
                c, at = u // top_owned, u % top_owned * nb
                at += c // parts * top_wide
                return halves[(c % parts - h) % parts][t, :, :, at : at + nb].reshape(nb, nb)

            def inv_dot(t, upper, r, out):
                a = halves[(upper - h) % parts][t, :, :, groups * top_wide :]
                out[t] = dot_t(a.reshape(nb, nb), r)

            for t in range(nt):
                r = r_scr[t]
                for u in range(t):
                    r = r - dot(q_block(t, u), y_scr[u])
                inv_dot(t, 0, r, y_scr)
            for t in range(nt - 1, -1, -1):
                r = y_scr[t]
                for u in range(t + 1, nt):
                    r = r - dot(q_block(t, u), x_ref[u])
                inv_dot(t, 1, r, x_ref)

        for h in range(parts):
            pl.when(grid.h == h)(functools.partial(solve, h))

    (top_x,) = call(
        top_body,
        after(pieces, [up[ds, 0] for ds in range(1, groups)]) + top_parts,
        [VMEM] * (nz + parts),
        [shaped(nt, nb, cols)],
        [VMEM],
        [pltpu.VMEM((nt, nz * rows, cols), F32), pltpu.VMEM((nt, nb, cols), F32)],
        "top_sweeps",
        20,
    )

    def couple_body(*refs):
        srcs, x_ref, mask = refs[:nsrc], refs[nsrc], refs[nsrc + 1]
        known = refs[nsrc + 2]
        tiles, sent, scr, m_scr, sem = refs[nsrc + 3 :]
        jobs = [
            (None, ref, scr.at[grid.block(ds, dh)]) for (ds, dh), ref in zip(grid.moves, srcs)
        ]
        start_all(jobs, sem)
        for t in range(nt):
            m_scr[pl.ds(t * nb, nb)] = x_ref[t] * mask[t]
        wait_all(jobs, sem)
        acc = None
        for c in range(nc):
            a = scr[c].reshape(count * rows, top_wide)
            term = dot(a, m_scr[pl.ds(c * top_wide, top_wide)])
            acc = term if acc is None else acc + term
        for i in range(count):
            tile = known[i] - acc[i * rows : (i + 1) * rows]
            tiles[i] = tile
            if i >= count - owned:
                sent[pl.ds((count - 1 - i) * rows, rows)] = tile

    tiles, sent = call(
        couple_body,
        [up[m] for m in grid.moves] + [top_x, present, lower_tiles],
        [VMEM] * nsrc + [VMEM, SMEM, VMEM],
        [shaped(count, rows, cols), shaped(owned * rows, cols)],
        [VMEM, VMEM],
        [
            pltpu.VMEM((nc, count, rows, top_wide), F32),
            pltpu.VMEM((nt * nb, cols), F32),
            pltpu.SemaphoreType.DMA((nsrc,)),
        ],
        "coupling",
        4,
    )

    def backward_stage(p, solved):
        g = nc - 1 - p
        nxt = [p * owned - 1 - n for n in range(owned)] if p else []
        known_ids = sorted(solved)
        ins = back + [solved[k] for k in known_ids]
        specs = [ANY] * parts + [VMEM] * len(known_ids)
        for i in nxt:
            ins += [a for a, _ in row_sources(i)]
            specs += [FREE] * nsrc
        if p:
            ins.append(tiles)
            specs.append(VMEM)
        size = per * part

        def body(*refs):
            inv = refs[:parts]
            known = []
            for k, ref in zip(known_ids, refs[parts : parts + len(known_ids)]):
                known += [(k * owned + n, ref.at[n]) for n in range(owned)]
            rest = refs[parts + len(known_ids) : len(ins)]
            outs = refs[len(ins) : -2]
            f_scr, sem = refs[-2:]
            jobs = [
                (None, inv[e].at[:, :, pl.ds(g * size, size)], outs[0].at[e]) for e in range(parts)
            ]
            for n, i in enumerate(nxt):
                jobs += fetch(i, rest[n * nsrc : (n + 1) * nsrc], f_scr, n)
            start_all(jobs, sem)
            wait_all(jobs, sem)
            for n, i in enumerate(nxt):
                outs[1][pl.ds(n * rows, rows)] = solved_sum(rest[-1][i], f_scr, n, known)
                outs[2][n] = f_scr[n, p]

        outs = [shaped(parts, nz, rows, size)]
        if p:
            outs += [shaped(owned * rows, cols), shaped(owned, rows, wide)]
        return call(
            body,
            ins,
            specs,
            outs,
            [VMEM] * len(outs),
            [
                pltpu.VMEM((owned, nc, rows, wide), F32),
                pltpu.SemaphoreType.DMA((owned * nsrc + parts,)),
            ],
            "backward_stage",
            1,
        )

    def backward_step(p, pieces, stage):
        ins = list(pieces) + list(stage)
        nout = 2 if p else 1

        def body(*refs):
            got, i_ref = refs[:nz], refs[nz]
            x_ref = refs[len(ins)]
            r_scr = refs[-1]
            for d in range(nz):
                for n in range(owned):
                    r_scr[n, rows_at(d)] = got[d][n * rows : (n + 1) * rows]
            at = owned * part
            for n in range(owned):
                for m in range(n):
                    for e in range(parts):
                        a = i_ref[e, :, :, at : at + part].reshape(nb, part)
                        half = pl.ds(pl.multiple_of(grid.part(e) * part, part), part)
                        r_scr[n] = r_scr[n] - dot(a, x_ref[owned - 1 - m, half])
                    at += part
                for e in range(parts):
                    a = i_ref[e, :, :, n * part : (n + 1) * part].reshape(nb, part)
                    half = pl.ds(pl.multiple_of(grid.part(e) * part, part), part)
                    x_ref[owned - 1 - n, half] = dot_t(a, r_scr[n])
            if p:
                for n in range(owned):
                    acc = refs[nz + 1][n * rows : (n + 1) * rows]
                    for m in range(owned):
                        a = refs[nz + 2][n, :, m * nb : (m + 1) * nb]
                        acc = acc - dot(a, x_ref[m])
                    refs[len(ins) + 1][pl.ds(n * rows, rows)] = acc

        res = call(
            body,
            ins,
            [VMEM] * len(ins),
            [shaped(owned, nb, cols), shaped(owned * rows, cols)][:nout],
            [VMEM] * nout,
            [pltpu.VMEM((owned, nz * rows, cols), F32)],
            "backward_step",
            5,
        )
        return res[0], res[1] if p else None

    def dest(ds, dh):
        return lax.rem(grid.s + (groups - ds), jnp.int32(groups)) * parts + lax.rem(
            grid.h + (parts - dh), jnp.int32(parts)
        )

    def plan_pairs(ins, outs):
        return [
            (dest(ds, dh) == p, ref, out)
            for (ds, dh), out in zip(grid.moves[1:], outs)
            for p, ref in enumerate(ins)
        ]

    solved, got_pairs = {}, {}
    for p in range(nc - 1, -1, -1):
        pieces = grid.gather_z(sent)
        stage = backward_stage(p, solved)
        solved[p], sent = backward_step(p, pieces, stage)
    pairs = move(
        [solved[q] for q in range(nc)],
        [shaped(owned, nb, cols)] * (nsrc - 1),
        plan_pairs,
        (nsrc - 1) * nc,
        "pack_pairs",
        near=True,
    )
    for m, x in reversed(list(zip(grid.moves[1:], pairs))):
        got_pairs[m] = grid.from_c(x, *m)

    def top_of(c):
        return lax.dynamic_slice_in_dim(top_x, c * top_owned, top_owned, 0)

    outs = [top_of(grid.c)]
    for e in range(1, parts):
        outs.append(grid.from_c(top_of(dest(0, e)), 0, e))
    outs = jnp.stack(outs)
    top_out = jnp.concatenate([pick(outs, (q - grid.h) % parts) for q in range(parts)], axis=2)
    top_out = lax.dynamic_slice_in_dim(top_out, grid.l * top_rhs.shape[2], top_rhs.shape[2], 2)

    def plan_out(ins, outs):
        jobs = []
        for n, (ds, dh) in enumerate(grid.moves):
            side = pl.ds(pl.multiple_of(grid.part(dh) * cols, cols), cols)
            target = outs[0].at[lax.rem(grid.s + ds, jnp.int32(groups)), :, :, side]
            if n == 0:
                jobs += [(grid.c == p, ins[p], target) for p in range(nc)]
            else:
                jobs.append((None, ins[nc + n - 1], target))
        return jobs

    ins = [solved[p] for p in range(nc)]
    for m in grid.moves[1:]:
        ins.append(got_pairs[m])
    def out_body(*refs):
        sem = refs[-1]
        jobs = plan_out(refs[: len(ins)], refs[len(ins) : -1])
        start_all(jobs, sem)
        wait_all(jobs, sem)

    (sub_out,) = call(
        out_body,
        ins,
        [VMEM] * len(ins),
        [shaped(groups, owned, nb, nrhs)],
        [ANY],
        [pltpu.SemaphoreType.DMA((len(ins),))],
        "place_out",
        1,
    )
    return (sub_out[None], top_out)


def solution(mesh):
    placed = (
        P("leaf", None, None, "prow", "pcol"),
        P("leaf", None, None, "prow", None),
        P("leaf", None, None, "prow", None),
        P("leaf", None, "prow", None, "pcol"),
        P("leaf", None, None, "prow", "pcol"),
        P("leaf", None, None),
        P(None, "prow", "pcol"),
        P(None, "prow", None),
        P(None, "prow", None),
        P("leaf", None, None, "prow", None),
        P(None, "prow", "leaf"),
    )
    return jax.shard_map(
        per_device,
        mesh=mesh,
        in_specs=placed,
        out_specs=(P("leaf", None, "pcol", None, None), P("pcol", None, "leaf")),
        check_vma=False,
    )
```

```python
import functools

import jax
import jax.numpy as jnp
from jax import lax
from jax.experimental import pallas as pl
from jax.experimental.pallas import tpu as pltpu
from jax.sharding import PartitionSpec as P

PRECISION = lax.Precision.HIGHEST
VMEM = pl.BlockSpec(memory_space=pltpu.VMEM)
SMEM = pl.BlockSpec(memory_space=pltpu.SMEM)
ANY = pl.BlockSpec(memory_space=pltpu.HBM)
FREE = pl.BlockSpec(memory_space=pltpu.HBM)
ARG = pl.BlockSpec(memory_space=pltpu.HBM)
F32 = jnp.float32
GRANT = 16 * 1024 * 1024


def dot(a, b):
    return lax.dot_general(
        a, b, (((1,), (0,)), ((), ())), precision=PRECISION, preferred_element_type=F32
    )


def dot_t(a, b):
    return lax.dot_general(
        a, b, (((0,), (0,)), ((), ())), precision=PRECISION, preferred_element_type=F32
    )


def shaped(*shape):
    return jax.ShapeDtypeStruct(shape, F32)


def after(x, dep):
    return x if dep is None else lax.optimization_barrier((x, dep))[0]


def pick(stack, index):
    return lax.dynamic_index_in_dim(stack, index, 0, keepdims=False)


class Grid:
    def __init__(self, groups, columns):
        self.nz = lax.axis_size("prow")
        self.nc = lax.axis_size("pcol")
        self.nl = lax.axis_size("leaf")
        self.groups = groups
        self.parts = self.nc // groups
        self.columns = columns // self.parts
        self.moves = [
            (ds, dh) for ds in range(groups) for dh in range(self.parts)
        ]

    @property
    def z(self):
        return lax.axis_index("prow")

    @property
    def c(self):
        return lax.axis_index("pcol")

    @property
    def l(self):
        return lax.axis_index("leaf")

    @property
    def s(self):
        return lax.div(self.c, jnp.int32(self.parts))

    @property
    def h(self):
        return lax.rem(self.c, jnp.int32(self.parts))

    def block(self, ds, dh):
        return lax.rem(self.s + ds, jnp.int32(self.groups)) * self.parts + self.part(dh)

    def part(self, dh):
        return lax.rem(self.h + dh, jnp.int32(self.parts))

    def row(self, d):
        return lax.rem(self.z + d, jnp.int32(self.nz))

    def from_z(self, x, d):
        return lax.ppermute(x, "prow", [((i + d) % self.nz, i) for i in range(self.nz)])

    def from_l(self, x, d):
        return lax.ppermute(x, "leaf", [((i + d) % self.nl, i) for i in range(self.nl)])

    def from_c(self, x, ds, dh):
        g, k = self.groups, self.parts
        return lax.ppermute(
            x,
            "pcol",
            [(((i // k + ds) % g) * k + (i % k + dh) % k, i) for i in range(self.nc)],
        )

    def gather_z(self, x):
        return [x] + [self.from_z(x, d) for d in range(1, self.nz)]


def call(body, ins, specs, outs, out_specs, scratch, name, us):
    ins = [
        pltpu.with_memory_space_constraint(x, pltpu.HBM) if spec in (ANY, ARG, FREE) else x
        for x, spec in zip(ins, specs)
    ]
    return pl.pallas_call(
        body,
        out_shape=tuple(
            pltpu.VMEM(o.shape, o.dtype) if spec is VMEM else o for o, spec in zip(outs, out_specs)
        ),
        in_specs=list(specs),
        out_specs=tuple(out_specs),
        scratch_shapes=list(scratch),
        compiler_params=pltpu.CompilerParams(vmem_limit_bytes=GRANT),
        cost_estimate=pl.CostEstimate(
            flops=int(us * 1.1e9), bytes_accessed=int(us * 3.6e6), transcendentals=0
        ),
        name=name,
    )(*ins)


def start_all(jobs, sem):
    for n, (cond, src, dst) in enumerate(jobs):
        copy = pltpu.make_async_copy(src, dst, sem.at[n])
        if cond is None:
            copy.start()
        else:
            pl.when(cond)(copy.start)


def wait_all(jobs, sem):
    for n, (cond, src, dst) in enumerate(jobs):
        copy = pltpu.make_async_copy(src, dst, sem.at[n])
        if cond is None:
            copy.wait()
        else:
            pl.when(cond)(copy.wait)


def move(ins, outs, plan, many, name, args=0, near=False):
    def body(*refs):
        sem = refs[-1]
        jobs = plan(refs[: len(ins)], refs[len(ins) : -1])
        start_all(jobs, sem)
        wait_all(jobs, sem)

    return call(
        body,
        ins,
        [ARG] * args + [VMEM if near else ANY] * (len(ins) - args),
        outs,
        [VMEM] * len(outs),
        [pltpu.SemaphoreType.DMA((many,))],
        name,
        1,
    )


def per_device(
    subtree_factor,
    sub_linv,
    sub_uinv,
    lower_panel,
    upper_panel,
    panel_rows,
    upper_level_factor,
    top_linv,
    top_uinv,
    sub_rhs,
    top_rhs,
):
    _, groups, count, rows, nrhs = sub_rhs.shape
    nb = sub_linv.shape[4]
    nt = top_rhs.shape[0]
    grid = Grid(groups, nrhs)
    nz, nc, nl, parts, cols = grid.nz, grid.nc, grid.nl, grid.parts, grid.columns
    owned = subtree_factor.shape[4] // nb
    top_owned = upper_level_factor.shape[2] // nb
    part = nb // parts
    wide = owned * nb
    early = count // 2
    share = nt * rows // nl
    piece = min(share, rows)
    top_wide = upper_level_factor.shape[2]
    top_pieces = top_wide // part
    cut = (count - early) * rows
    factor, linv, uinv = subtree_factor[0], sub_linv[0], sub_uinv[0]
    rhs = sub_rhs[0]

    def own_part(width):
        return pl.ds(pl.multiple_of(grid.h * width, width), width)

    def rows_at(d):
        return pl.ds(pl.multiple_of(grid.row(d) * rows, rows), rows)

    order = list(range(1, count)) + [0]
    chunks = [order[:owned], order[owned : 2 * owned], order[2 * owned :]]
    where = {i: (n, k) for n, chunk in enumerate(chunks) for k, i in enumerate(chunk)}

    def other(ds):
        return lax.rem(grid.s + (groups - ds), jnp.int32(groups))

    def plan_first(ins, outs):
        rhs_, linv_, factor_ = ins
        m0 = outs[0]
        jobs = [
            (None, rhs_.at[grid.s, 0, :, own_part(cols)], m0.at[:, pl.ds(0, cols)]),
            (None, linv_.at[grid.s, 0], m0.at[:, pl.ds(cols, nb)]),
        ]
        for i in range(1, early):
            at = pl.ds(cols + nb + (i - 1) * part, part)
            jobs.append((None, linv_.at[grid.s, i, :, own_part(part)], m0.at[:, at]))
        for ds in range(1, groups):
            for k, i in enumerate(chunks[0]):
                jobs.append((None, factor_.at[other(ds), i], outs[ds].at[k]))
        return jobs

    first = move(
        [rhs, linv, factor],
        [shaped(rows, cols + nb + (early - 1) * part)]
        + [shaped(owned, rows, wide)] * (groups - 1),
        plan_first,
        1 + early + (groups - 1) * owned,
        "pack_first",
        args=3,
    )
    m0 = grid.gather_z(first[0])
    y_got, sources = {}, {}
    for ds in range(1, groups):
        y_got[ds, 0] = grid.from_c(first[ds], ds, 0)

    def plan_second(ins, outs):
        jobs = [(None, ins[0].at[grid.s], outs[0])]
        for ds in range(1, groups):
            for n in range(1, len(chunks)):
                target = outs[(ds - 1) * (len(chunks) - 1) + n]
                for k, i in enumerate(chunks[n]):
                    jobs.append((None, ins[0].at[other(ds), i], target.at[k]))
        return jobs

    second = move(
        [after(factor, first[0])],
        [shaped(count, rows, wide)]
        + [shaped(len(chunk), rows, wide) for chunk in chunks[1:]] * (groups - 1),
        plan_second,
        1 + count * groups,
        "pack_second",
        args=1,
    )
    own = second[0]

    def plan_bulk(ins, outs):
        linv_, top_, tl_, tu_ = ins
        bulk = outs[0]
        jobs = []
        for k in range(count - early):
            jobs.append(
                (
                    None,
                    linv_.at[grid.s, early + k, :, own_part(part)],
                    bulk.at[pl.ds(k * rows, rows)],
                )
            )
        for a in range(share // piece):
            flat = grid.l * share + a * piece
            t = lax.div(flat, jnp.int32(rows))
            at = pl.ds(pl.multiple_of(lax.rem(flat, jnp.int32(rows)), piece), piece)
            for n in range(top_pieces + 1):
                target = bulk.at[pl.ds(cut + n * share + a * piece, piece)]
                if n < top_pieces:
                    jobs.append((None, top_.at[t, at, pl.ds(n * part, part)], target))
                    continue
                low = pl.ds(pl.multiple_of(grid.s * part, part), part)
                jobs.append((grid.h == 0, tl_.at[t, at, low], target))
                jobs.append((grid.h == 1, tu_.at[t, at, low], target))
        return jobs

    (bulk,) = move(
        [linv, upper_level_factor, top_linv, top_uinv],
        [shaped(cut + (top_pieces + 1) * share, part)],
        plan_bulk,
        count - early + (top_pieces + 2) * (share // piece),
        "pack_bulk",
        args=4,
    )
    gathered = lax.all_gather(after(bulk, m0), "prow")

    def plan_core(ins, outs):
        jobs = [(None, ins[0].at[chunks[0][0]], outs[0].at[0])]
        for ds in range(1, groups):
            jobs.append((None, ins[ds], outs[0].at[pl.ds(1 + (ds - 1) * owned, owned)]))
        return jobs

    (core,) = move(
        [own] + after([y_got[ds, 0] for ds in range(1, groups)], (m0, bulk)),
        [shaped(1 + (groups - 1) * owned, rows, wide)],
        plan_core,
        groups,
        "pack_core",
        near=True,
    )
    cores = {dh: grid.from_c(core, 0, dh) for dh in range(1, parts)}

    def start_chunk(n, dep):
        for ds in range(1, groups):
            sent = second[(ds - 1) * (len(chunks) - 1) + n]
            y_got[ds, n] = grid.from_c(after(sent, dep), ds, 0)
        return [y_got[ds, n] for ds in range(1, groups)]

    def share_chunk(n, dep):
        for ds in range(1, groups):
            for dh in range(1, parts):
                y_got[ds, dh, n] = grid.from_c(after(y_got[ds, n], dep), 0, dh)

    def row_sources(i):
        n, k = where[i]
        out = []
        for ds, dh in grid.moves:
            if dh == 0:
                out.append((y_got[ds, n], k) if ds else (own, i))
            elif n == 0 and ds:
                out.append((cores[dh], 1 + (ds - 1) * owned + k))
            elif ds:
                out.append((y_got[ds, dh, n], k))
            else:
                out.append((cores[dh], 0) if i == chunks[0][0] else (sources[0, dh], i))
        return out

    early_inv = []

    def plan_late(ins, outs):
        jobs = [
            (
                None,
                ins[0].at[a, pl.ds(k * rows, rows)],
                outs[0].at[k, pl.ds(a * rows, rows)],
            )
            for a in range(nz)
            for k in range(count - early)
        ]
        size = (top_pieces + 1) * share
        return jobs + [(None, ins[0].at[:, pl.ds(cut, size)], outs[1])]

    late_inv = []

    def place_late(dep):
        mine, top_mine = move(
            [after(gathered, dep)],
            [
                shaped(count - early, nz * rows, part),
                shaped(nz, (top_pieces + 1) * share, part),
            ],
            plan_late,
            nz * (count - early) + 1,
            "place_late",
        )
        late_inv.extend([mine] + [grid.from_c(mine, 0, dh) for dh in range(1, parts)])
        return top_mine

    def inverse_of(i):
        if i < early:
            return early_inv, i - 1
        return late_inv, i - early

    def fetch(i, refs, scratch, slot):
        return [
            (None, ref.at[index], scratch.at[slot, grid.block(ds, dh)])
            for (ds, dh), ref, (_, index) in zip(grid.moves, refs, row_sources(i))
        ]

    def solved_sum(acc, scratch, slot, known):
        for k, x in known:
            acc = acc - dot(
                scratch[slot, k // owned, :, (k % owned) * nb : (k % owned + 1) * nb], x[...]
            )
        return acc

    nsrc = len(grid.moves)

    def forward_step(i, pieces, solved, extra=()):
        last = i == count - 1
        solved = [] if last else solved
        ins, specs = list(pieces), [VMEM] * nz
        if i:
            stack, index = inverse_of(i)
            ins += stack
            specs += [FREE] * parts
        ninv = len(ins) - nz
        ins += solved
        specs += [VMEM] * len(solved)
        if last:
            ins += list(extra)
            specs += [VMEM, VMEM, SMEM] + [ANY] * nsrc
        else:
            ins += [a for a, _ in row_sources(i + 1)] + [rhs]
            specs += [FREE] * nsrc + [ARG]

        def body(*refs):
            got = refs[:nz]
            inv = refs[nz : nz + ninv]
            known = refs[nz + ninv : nz + ninv + len(solved)]
            rest = refs[nz + ninv + len(solved) : len(ins)]
            x_ref, next_ref = refs[len(ins) : len(ins) + 2]
            r_scr, i_scr, f_scr, t_scr, p_scr, sem, i_sem = refs[-7:]
            inv_jobs = [
                (None, inv[e].at[index], i_scr.at[:, pl.ds(e * part, part)]) for e in range(ninv)
            ]
            start_all(inv_jobs, i_sem)
            if last:
                jobs = [
                    (
                        grid.block(ds, dh) == nc - 1,
                        ref.at[:, pl.ds((owned - 1) * nb, nb)],
                        p_scr,
                    )
                    for (ds, dh), ref in zip(grid.moves, rest[3:])
                ]
                start_all(jobs, sem)
            else:
                jobs = fetch(i + 1, rest[:nsrc], f_scr, 0)
                jobs.append((None, rest[nsrc].at[grid.s, i + 1, :, own_part(cols)], t_scr))
                start_all(jobs, sem)
            for d in range(nz):
                r_scr[rows_at(d)] = got[d][:, :cols]
                if i == 0:
                    i_scr[rows_at(d)] = got[d][:, cols : cols + nb]
                    for k in range(early - 1):
                        at = cols + nb + k * part
                        refs[len(ins) + 2][k, rows_at(d)] = got[d][:, at : at + part]
            if i == 0:
                x_ref[...] = dot_t(i_scr[...], r_scr[...])
            wait_all(inv_jobs, i_sem)
            for e in range(ninv):
                at = pl.ds(pl.multiple_of(grid.part(e) * part, part), part)
                x_ref[at] = dot_t(i_scr[:, e * part : (e + 1) * part], r_scr[...])
            if last:
                wait_all(jobs, sem)
                total = rest[0][...] + dot(p_scr[...], x_ref[...])
                for t in range(nt):
                    at = slice(t * rows, (t + 1) * rows)
                    next_ref[at] = rest[1][at] - total[at] * rest[2][t]
            else:
                wait_all(jobs, sem)
                known = list(enumerate(known)) + [(i, x_ref)]
                next_ref[...] = solved_sum(t_scr[...], f_scr, 0, known)

        return call(
            body,
            ins,
            specs,
            [shaped(nb, cols), shaped(nt * rows if last else rows, cols)]
            + [shaped(early - 1, nz * rows, part)] * (i == 0),
            [VMEM] * (2 + (i == 0)),
            [
                pltpu.VMEM((nz * rows, cols), F32),
                pltpu.VMEM((nz * rows, nb), F32),
                pltpu.VMEM((1, nc, rows, wide), F32),
                pltpu.VMEM((rows, cols), F32),
                pltpu.VMEM((nt * rows, nb) if last else (rows, nb), F32),
                pltpu.SemaphoreType.DMA((nsrc + 1,)),
                pltpu.SemaphoreType.DMA((parts,)),
            ],
            "forward_step",
            4,
        )

    def forward_stage(i, solved):
        last = i == count - 1
        stack, index = inverse_of(i)
        ins, specs = list(stack), [FREE] * parts
        if last:
            ins += [lp[m] for m in grid.moves]
            specs += [ANY] * nsrc
        else:
            ins += solved + [a for a, _ in row_sources(i + 1)] + [rhs]
            specs += [VMEM] * len(solved) + [FREE] * nsrc + [ARG]

        def body(*refs):
            rest = refs[parts : len(ins)]
            inv_ref, new_ref = refs[len(ins) : len(ins) + 2]
            f_scr, t_scr, sem = refs[-3:]
            jobs = [
                (None, refs[e].at[index], inv_ref.at[:, pl.ds(e * part, part)])
                for e in range(parts)
            ]
            if last:
                at = pl.ds((owned - 1) * nb, nb)
                jobs += [
                    (grid.block(*m) == nc - 1, ref.at[:, at], new_ref)
                    for m, ref in zip(grid.moves, rest)
                ]
            else:
                jobs += fetch(i + 1, rest[len(solved) : -1], f_scr, 0)
                jobs.append((None, rest[-1].at[grid.s, i + 1, :, own_part(cols)], t_scr))
            start_all(jobs, sem)
            wait_all(jobs, sem)
            if not last:
                known = list(enumerate(rest[: len(solved)]))
                refs[len(ins) + 2][...] = solved_sum(t_scr[...], f_scr, 0, known)
                new_ref[...] = f_scr[0, i // owned, :, (i % owned) * nb : (i % owned + 1) * nb]

        outs = [shaped(nz * rows, nb)]
        if last:
            outs.append(shaped(nt * rows, nb))
        else:
            outs += [shaped(rows, nb), shaped(rows, cols)]
        return call(
            body,
            ins,
            specs,
            outs,
            [VMEM] * len(outs),
            [
                pltpu.VMEM((1, nc, rows, wide), F32),
                pltpu.VMEM((rows, cols), F32),
                pltpu.SemaphoreType.DMA((nsrc + 1 + parts,)),
            ],
            "forward_stage",
            1,
        )

    def forward_solve(i, pieces, stage, extra=()):
        last = i == count - 1
        ins = list(pieces) + list(stage) + list(extra)
        specs = [VMEM] * (nz + len(stage)) + [VMEM, VMEM, SMEM] * last

        def body(*refs):
            got, inv_ref, new_ref = refs[:nz], refs[nz], refs[nz + 1]
            rest = refs[nz + 2 : len(ins)]
            x_ref, next_ref, r_scr = refs[len(ins) :]
            for d in range(nz):
                r_scr[rows_at(d)] = got[d][...]
            for e in range(parts):
                at = pl.ds(pl.multiple_of(grid.part(e) * part, part), part)
                x_ref[at] = dot_t(inv_ref[:, e * part : (e + 1) * part], r_scr[...])
            if last:
                total = rest[0][...] + dot(new_ref[...], x_ref[...])
                for t in range(nt):
                    at = slice(t * rows, (t + 1) * rows)
                    next_ref[at] = rest[1][at] - total[at] * rest[2][t]
            else:
                next_ref[...] = rest[0][...] - dot(new_ref[...], x_ref[...])

        return call(
            body,
            ins,
            specs,
            [shaped(nb, cols), shaped(nt * rows if last else rows, cols)],
            [VMEM] * 2,
            [pltpu.VMEM((nz * rows, cols), F32)],
            "forward_solve",
            2,
        )

    present = lax.dynamic_index_in_dim(panel_rows[0].astype(F32), grid.s, 1, keepdims=False)
    per = owned * (owned + 1) // 2
    def plan_back(ins, outs):
        out = outs[0]
        jobs = []
        for p in range(nc):
            base = (nc - 1 - p) * per * part
            for n in range(owned):
                jobs.append(
                    (
                        None,
                        ins[0].at[grid.s, p * owned + owned - 1 - n, :, own_part(part)],
                        out.at[:, pl.ds(base + n * part, part)],
                    )
                )
        at = 1
        for ds, dh in grid.moves:
            p = grid.block(ds, dh)
            col = pl.ds(pl.multiple_of(nb + grid.h * part, part), part)
            to = pl.ds(pl.multiple_of((nc - 1 - p) * per * part + owned * part, part), part)
            if ds == 0:
                jobs.append((None, ins[at].at[p * owned, :, col], out.at[:, to]))
                at += 1
                continue
            for q in range(nc):
                n, k = where[q * owned]
                if dh and not n:
                    k += 1 + (ds - 1) * owned
                jobs.append((p == q, ins[at + n].at[k, :, col], out.at[:, to]))
            at += len(chunks)
        return jobs

    def pack_back():
        ins = [after(uinv, lower[2])]
        for ds, dh in grid.moves:
            if ds == 0:
                ins.append(own if dh == 0 else sources[0, dh])
            else:
                for n in range(len(chunks)):
                    if dh == 0:
                        ins.append(y_got[ds, n])
                    else:
                        ins.append(y_got[ds, dh, n] if n else cores[dh])
        (back,) = move(
            ins, [shaped(rows, nc * per * part)], plan_back, nc * owned + nsrc * nc, "pack_back", args=1
        )
        return back

    def top_side(dep):
        width = top_rhs.shape[2]
        start = grid.l * width - grid.h * cols
        held = jnp.logical_and(grid.s == 0, jnp.logical_and(start >= 0, start < cols))
        mine = jnp.where(held, after(top_rhs, dep), 0.0)
        if width < cols:
            blank = jnp.zeros((nt, rows, cols), F32)
            at = jnp.clip(start, 0, cols - width)
            mine = lax.dynamic_update_slice_in_dim(blank, mine, at, 2)
        return mine.reshape(nt * rows, cols)

    group_wide = top_wide + part

    def place_top(dep):
        keys = sorted(top_got)

        def plan_top(ins, outs):
            jobs = []
            for (dl, ds), ref in zip(keys, ins):
                sg = lax.rem(grid.s + ds, jnp.int32(groups))
                flat = lax.rem(grid.l + dl, jnp.int32(nl)) * share
                for a in range(share // piece):
                    at = flat + a * piece
                    t = lax.div(at, jnp.int32(rows))
                    r0 = pl.ds(pl.multiple_of(lax.rem(at, jnp.int32(rows)), piece), piece)
                    for n in range(top_pieces + 1):
                        src = ref.at[:, pl.ds(n * share + a * piece, piece)]
                        col = sg * top_wide + n * part
                        if n == top_pieces:
                            col = groups * top_wide + sg * part
                        col = pl.ds(pl.multiple_of(col, part), part)
                        jobs.append((None, src, outs[0].at[t, :, r0, col]))
            return jobs

        return move(
            after([top_got[k] for k in keys], dep),
            [shaped(nt, nz, rows, groups * group_wide)],
            plan_top,
            nl * groups * (share // piece) * (top_pieces + 1),
            "place_top",
            near=True,
        )[0]

    def pack_upper(dep):
        def plan_upper(ins, outs):
            return [(None, ins[0].at[grid.s], outs[0])] + [
                (None, ins[0].at[other(ds)], outs[ds]) for ds in range(1, groups)
            ]

        return move(
            [after(upper_panel[0], dep)],
            [shaped(count, rows, top_wide)] * groups,
            plan_upper,
            groups,
            "pack_upper",
            args=1,
        )

    lower = []
    lp, top_got = {}, {}
    panel = lower_panel[0]

    def panel_of(s, dep):
        x = lax.dynamic_index_in_dim(panel, after(s, dep), 2, keepdims=False)
        return x.reshape(nt * rows, wide)

    pieces = m0
    for i in range(count):
        due = []
        if i == 0:
            for dh in range(1, parts):
                sources[0, dh] = grid.from_c(own, 0, dh)
                due.append(sources[0, dh])
        if i == 1:
            early_inv.extend(
                [mine_early] + [grid.from_c(mine_early, 0, dh) for dh in range(1, parts)]
            )
            due += start_chunk(1, lower[0])
        if i == 2:
            share_chunk(1, lower[1])
            in_flight = start_chunk(2, lower[1])
        if i == early - 1:
            due += in_flight
            share_chunk(2, lower[-1])
            top_mine = place_late((lower[-1], pieces))
            top_got[0, 0] = top_mine
        if i == early:
            held = (lower[-1], late_inv, [v for k, v in y_got.items() if len(k) == 3])
            for dl in range(1, nl):
                top_got[dl, 0] = grid.from_l(after(top_mine, held), dl)
            for ds in range(1, groups):
                top_got[0, ds] = grid.from_c(after(top_mine, held), ds, 0)
        if i == early - 2:
            side = top_side(lower[-1])
        if i == early + 1:
            due += [top_got[k] for k in top_got if any(k)]
            back = pack_back()
            due.append(back)
            back = lax.all_gather(back, "prow")
        if i == early + 2:
            for ds in range(1, groups):
                for dl in range(1, nl):
                    top_got[dl, ds] = grid.from_l(after(top_got[0, ds], lower[-1]), dl)
            lp[0, 0] = panel_of(grid.s, lower[2])
            for ds in range(1, groups):
                lp[ds, 0] = grid.from_c(after(panel_of(other(ds), lower[2]), lower[-1]), ds, 0)
            due += [lp[ds, 0] for ds in range(1, groups)]
        if i == count - 1:
            due.append(back)
            ups = pack_upper(lower[-1])
            due += list(ups)
        pieces = after(pieces, due)
        if i == count - 1:
            def panel_body(*refs):
                srcs, known = refs[:nsrc], refs[nsrc : nsrc + count - 1]
                total, scr, sem = refs[nsrc + count - 1 :]
                jobs = [
                    (None, ref, scr.at[grid.block(ds, dh)])
                    for (ds, dh), ref in zip(grid.moves, srcs)
                ]
                start_all(jobs, sem)
                wait_all(jobs, sem)
                acc = None
                for k, x in enumerate(known):
                    a = scr[k // owned, :, (k % owned) * nb : (k % owned + 1) * nb]
                    term = dot(a, x[...])
                    acc = term if acc is None else acc + term
                total[...] = acc

            for ds in range(groups):
                for dh in range(1, parts):
                    lp[ds, dh] = grid.from_c(after(lp[ds, 0], lower[-1]), 0, dh)
            (total,) = call(
                panel_body,
                [lp[m] for m in grid.moves] + lower,
                [ANY] * nsrc + [VMEM] * (count - 1),
                [shaped(nt * rows, cols)],
                [VMEM],
                [pltpu.VMEM((nc, nt * rows, wide), F32), pltpu.SemaphoreType.DMA((nsrc,))],
                "panel_sums",
                3,
            )
            stage = forward_stage(i, lower)
            x, contrib = forward_solve(i, pieces, stage, [total, side, present])
        else:
            if i:
                x, sent = forward_solve(i, pieces, forward_stage(i, lower))
            else:
                x, sent, *rest = forward_step(i, pieces, lower)
            if i == 0:
                mine_early = rest[0]
            pieces = grid.gather_z(sent)
        lower.append(x)


    def tiles_body(*refs):
        for i in range(count):
            refs[count][i] = refs[i][rows_at(0)]

    (lower_tiles,) = call(
        tiles_body,
        lower[:-1] + [after(lower[-1], contrib)],
        [VMEM] * count,
        [shaped(count, rows, cols)],
        [VMEM],
        [],
        "row_tiles",
        1,
    )
    total, arrived = contrib, []
    if nl * groups <= 4:
        for dl in range(nl):
            for ds in range(groups):
                if dl or ds:
                    pairs = [
                        (
                            ((j + dl) % nl) * nc
                            + ((c // parts + ds) % groups) * parts
                            + c % parts,
                            j * nc + c,
                        )
                        for j in range(nl)
                        for c in range(nc)
                    ]
                    arrived.append(lax.ppermute(contrib, ("leaf", "pcol"), pairs))
        for x in arrived:
            total = total + x
    else:
        for ds in range(1, groups):
            total = total + grid.from_c(contrib, ds, 0)
        total = lax.psum(total, "leaf")
    up = {(0, 0): ups[0]}

    sent = after(total, lower_tiles)
    for ds in range(1, groups):
        up[ds, 0] = grid.from_c(after(ups[ds], sent), ds, 0)
    top_half = place_top(sent)
    top_parts = [top_half] + [grid.from_c(top_half, 0, dh) for dh in range(1, parts)]
    pieces = grid.gather_z(after(sent, top_half))
    back = after(back, sent)
    back = [back] + [grid.from_c(back, 0, dh) for dh in range(1, parts)]
    for ds in range(groups):
        for dh in range(1, parts):
            up[ds, dh] = grid.from_c(after(up[ds, 0], pieces), 0, dh)

    def top_body(*refs):
        got = refs[:nz]
        halves = refs[nz : nz + parts]
        x_ref, r_scr, y_scr = refs[nz + parts :]
        for d in range(nz):
            for t in range(nt):
                r_scr[t, rows_at(d)] = got[d][t * rows : (t + 1) * rows]

        def solve(h):
            def q_block(t, u):
                c, at = u // top_owned, u % top_owned * nb
                at += c // parts * top_wide
                return halves[(c % parts - h) % parts][t, :, :, at : at + nb].reshape(nb, nb)

            def inv_dot(t, upper, r, out):
                a = halves[(upper - h) % parts][t, :, :, groups * top_wide :]
                out[t] = dot_t(a.reshape(nb, nb), r)

            for t in range(nt):
                r = r_scr[t]
                for u in range(t):
                    r = r - dot(q_block(t, u), y_scr[u])
                inv_dot(t, 0, r, y_scr)
            for t in range(nt - 1, -1, -1):
                r = y_scr[t]
                for u in range(t + 1, nt):
                    r = r - dot(q_block(t, u), x_ref[u])
                inv_dot(t, 1, r, x_ref)

        for h in range(parts):
            pl.when(grid.h == h)(functools.partial(solve, h))

    (top_x,) = call(
        top_body,
        after(pieces, [up[ds, 0] for ds in range(1, groups)]) + top_parts,
        [VMEM] * (nz + parts),
        [shaped(nt, nb, cols)],
        [VMEM],
        [pltpu.VMEM((nt, nz * rows, cols), F32), pltpu.VMEM((nt, nb, cols), F32)],
        "top_sweeps",
        20,
    )

    def couple_body(*refs):
        srcs, x_ref, mask = refs[:nsrc], refs[nsrc], refs[nsrc + 1]
        known = refs[nsrc + 2]
        tiles, sent, scr, m_scr, sem = refs[nsrc + 3 :]
        jobs = [
            (None, ref, scr.at[grid.block(ds, dh)]) for (ds, dh), ref in zip(grid.moves, srcs)
        ]
        start_all(jobs, sem)
        for t in range(nt):
            m_scr[pl.ds(t * nb, nb)] = x_ref[t] * mask[t]
        wait_all(jobs, sem)
        acc = None
        for c in range(nc):
            a = scr[c].reshape(count * rows, top_wide)
            term = dot(a, m_scr[pl.ds(c * top_wide, top_wide)])
            acc = term if acc is None else acc + term
        for i in range(count):
            tile = known[i] - acc[i * rows : (i + 1) * rows]
            tiles[i] = tile
            if i >= count - owned:
                sent[pl.ds((count - 1 - i) * rows, rows)] = tile

    tiles, sent = call(
        couple_body,
        [up[m] for m in grid.moves] + [top_x, present, lower_tiles],
        [VMEM] * nsrc + [VMEM, SMEM, VMEM],
        [shaped(count, rows, cols), shaped(owned * rows, cols)],
        [VMEM, VMEM],
        [
            pltpu.VMEM((nc, count, rows, top_wide), F32),
            pltpu.VMEM((nt * nb, cols), F32),
            pltpu.SemaphoreType.DMA((nsrc,)),
        ],
        "coupling",
        4,
    )

    def backward_stage(p, solved):
        g = nc - 1 - p
        nxt = [p * owned - 1 - n for n in range(owned)] if p else []
        known_ids = sorted(solved)
        ins = back + [solved[k] for k in known_ids]
        specs = [ANY] * parts + [VMEM] * len(known_ids)
        for i in nxt:
            ins += [a for a, _ in row_sources(i)]
            specs += [FREE] * nsrc
        if p:
            ins.append(tiles)
            specs.append(VMEM)
        size = per * part

        def body(*refs):
            inv = refs[:parts]
            known = []
            for k, ref in zip(known_ids, refs[parts : parts + len(known_ids)]):
                known += [(k * owned + n, ref.at[n]) for n in range(owned)]
            rest = refs[parts + len(known_ids) : len(ins)]
            outs = refs[len(ins) : -2]
            f_scr, sem = refs[-2:]
            jobs = [
                (None, inv[e].at[:, :, pl.ds(g * size, size)], outs[0].at[e]) for e in range(parts)
            ]
            for n, i in enumerate(nxt):
                jobs += fetch(i, rest[n * nsrc : (n + 1) * nsrc], f_scr, n)
            start_all(jobs, sem)
            wait_all(jobs, sem)
            for n, i in enumerate(nxt):
                outs[1][pl.ds(n * rows, rows)] = solved_sum(rest[-1][i], f_scr, n, known)
                outs[2][n] = f_scr[n, p]

        outs = [shaped(parts, nz, rows, size)]
        if p:
            outs += [shaped(owned * rows, cols), shaped(owned, rows, wide)]
        return call(
            body,
            ins,
            specs,
            outs,
            [VMEM] * len(outs),
            [
                pltpu.VMEM((owned, nc, rows, wide), F32),
                pltpu.SemaphoreType.DMA((owned * nsrc + parts,)),
            ],
            "backward_stage",
            1,
        )

    def backward_step(p, pieces, stage):
        ins = list(pieces) + list(stage)
        nout = 2 if p else 1

        def body(*refs):
            got, i_ref = refs[:nz], refs[nz]
            x_ref = refs[len(ins)]
            r_scr = refs[-1]
            for d in range(nz):
                for n in range(owned):
                    r_scr[n, rows_at(d)] = got[d][n * rows : (n + 1) * rows]
            at = owned * part
            for n in range(owned):
                for m in range(n):
                    for e in range(parts):
                        a = i_ref[e, :, :, at : at + part].reshape(nb, part)
                        half = pl.ds(pl.multiple_of(grid.part(e) * part, part), part)
                        r_scr[n] = r_scr[n] - dot(a, x_ref[owned - 1 - m, half])
                    at += part
                for e in range(parts):
                    a = i_ref[e, :, :, n * part : (n + 1) * part].reshape(nb, part)
                    half = pl.ds(pl.multiple_of(grid.part(e) * part, part), part)
                    x_ref[owned - 1 - n, half] = dot_t(a, r_scr[n])
            if p:
                for n in range(owned):
                    acc = refs[nz + 1][n * rows : (n + 1) * rows]
                    for m in range(owned):
                        a = refs[nz + 2][n, :, m * nb : (m + 1) * nb]
                        acc = acc - dot(a, x_ref[m])
                    refs[len(ins) + 1][pl.ds(n * rows, rows)] = acc

        res = call(
            body,
            ins,
            [VMEM] * len(ins),
            [shaped(owned, nb, cols), shaped(owned * rows, cols)][:nout],
            [VMEM] * nout,
            [pltpu.VMEM((owned, nz * rows, cols), F32)],
            "backward_step",
            5,
        )
        return res[0], res[1] if p else None

    def dest(ds, dh):
        return lax.rem(grid.s + (groups - ds), jnp.int32(groups)) * parts + lax.rem(
            grid.h + (parts - dh), jnp.int32(parts)
        )

    def plan_pairs(ins, outs):
        return [
            (dest(ds, dh) == p, ref, out)
            for (ds, dh), out in zip(grid.moves[1:], outs)
            for p, ref in enumerate(ins)
        ]

    solved, got_pairs = {}, {}
    for p in range(nc - 1, -1, -1):
        pieces = grid.gather_z(sent)
        stage = backward_stage(p, solved)
        solved[p], sent = backward_step(p, pieces, stage)
    pairs = move(
        [solved[q] for q in range(nc)],
        [shaped(owned, nb, cols)] * (nsrc - 1),
        plan_pairs,
        (nsrc - 1) * nc,
        "pack_pairs",
        near=True,
    )
    for m, x in reversed(list(zip(grid.moves[1:], pairs))):
        got_pairs[m] = grid.from_c(x, *m)

    def top_of(c):
        return lax.dynamic_slice_in_dim(top_x, c * top_owned, top_owned, 0)

    outs = [top_of(grid.c)]
    for e in range(1, parts):
        outs.append(grid.from_c(top_of(dest(0, e)), 0, e))
    outs = jnp.stack(outs)
    top_out = jnp.concatenate([pick(outs, (q - grid.h) % parts) for q in range(parts)], axis=2)
    top_out = lax.dynamic_slice_in_dim(top_out, grid.l * top_rhs.shape[2], top_rhs.shape[2], 2)

    def plan_out(ins, outs):
        jobs = []
        for n, (ds, dh) in enumerate(grid.moves):
            side = pl.ds(pl.multiple_of(grid.part(dh) * cols, cols), cols)
            target = outs[0].at[lax.rem(grid.s + ds, jnp.int32(groups)), :, :, side]
            if n == 0:
                jobs += [(grid.c == p, ins[p], target) for p in range(nc)]
            else:
                jobs.append((None, ins[nc + n - 1], target))
        return jobs

    ins = [solved[p] for p in range(nc)]
    for m in grid.moves[1:]:
        ins.append(got_pairs[m])
    def out_body(*refs):
        sem = refs[-1]
        jobs = plan_out(refs[: len(ins)], refs[len(ins) : -1])
        start_all(jobs, sem)
        wait_all(jobs, sem)

    (sub_out,) = call(
        out_body,
        ins,
        [VMEM] * len(ins),
        [shaped(groups, owned, nb, nrhs)],
        [ANY],
        [pltpu.SemaphoreType.DMA((len(ins),))],
        "place_out",
        1,
    )
    return (sub_out[None], top_out)


def solution(mesh):
    placed = (
        P("leaf", None, None, "prow", "pcol"),
        P("leaf", None, None, "prow", None),
        P("leaf", None, None, "prow", None),
        P("leaf", None, "prow", None, "pcol"),
        P("leaf", None, None, "prow", "pcol"),
        P("leaf", None, None),
        P(None, "prow", "pcol"),
        P(None, "prow", None),
        P(None, "prow", None),
        P("leaf", None, None, "prow", None),
        P(None, "prow", "leaf"),
    )
    return jax.shard_map(
        per_device,
        mesh=mesh,
        in_specs=placed,
        out_specs=(P("leaf", None, "pcol", None, None), P("pcol", None, "leaf")),
        check_vma=False,
    )
```
